128 devices in a mesh: seq: 4 (over y_hi, core), mp: 32 (over x, y_lo, z).
Axes of the slice: x: 4, y: 4 (y_hi: 2, y_lo: 2; y = y_hi * 2 + y_lo), z: 4, core: 2. Of those that a mesh axis runs over, the one named last changes fastest.
Arguments:
- queries: bfloat16 [1024, 8192], P('seq', 'mp'), may hold values from -32 to 32
- new_kv: bfloat16 [2, 1024, 512], P(None, 'seq'), may hold values from -6 to 6
- cache_kv: bfloat16 [2, 8192, 512], P(None, 'seq'), may hold values from -6 to 6
- cached_len: int32 [1], replicated, may hold values from 4096 to 8192
- image_spans: int32 [3, 2], replicated, may hold values from 0 to 1024, as said below
- residual: bfloat16 [1024, 4096], P(('seq', 'mp')), may hold values from -4 to 4
- out_proj: bfloat16 [8192, 4096], P('mp'), may hold values from -0.0625 to 0.0625
- norm_gain: float32 [4096], replicated, may hold values from 0.5 to 1.5
- routes: int32 [1024, 8], P(('seq', 'mp')), may hold values from 0 to 63, all different within a row; in each aligned block of 8 rows (0 to 7, 8 to 15, ...) at most 2 rows name the same one
- gate_weights: float32 [1024, 8], P(('seq', 'mp')), may hold values from 0.05 to 1
- w_in: bfloat16 [64, 4096, 2, 1536], P('mp', None, None, 'seq'), may hold values from -0.09375 to 0.09375
- w_out: bfloat16 [64, 1536, 4096], P('mp', 'seq'), may hold values from -0.15625 to 0.15625
Outputs:
- mixed: bfloat16 [1024, 4096], P(('seq', 'mp'))
The draws below stay inside these ranges and needn't reach their ends.
Inputs may be any that keep to these rules, and one draw needn't show every extreme that they name: `image_spans`: each row is an image span [start, end) of tract positions; rows are in increasing order, disjoint and nonempty. `routes`: each row names 8 different experts; within the rows of one device (aligned blocks of 8 rows) no expert is named more than 2 times.
All inputs are finite; a program needn't handle non-finite values.
Results may differ from the reference program's by a relative error of at most 0.025.
Values may be sent and summed in bfloat16 or wider, within the bound.
No kernel may reach another device: no remote copies, remote signals or barrier semaphores. Data moves between devices by JAX's collectives and lax.ppermute only.
A program may use at most 128 MiB of HBM per device.

```python
import math
import jax
import jax.numpy as jnp
import numpy as np
from jax import lax

D = 4096
HEADS = 64
KV_HEADS = 4
HEAD_DIM = 128
FF = 1536
TOP = 8
SPANS = 3
EXPERTS = 64
TRACT = 1024
CACHE = 8192
HEADS_DEV = 2
FF_DEV = 384
TOK_MOE = 8
CAP = 2
N_SEQ = 4
N_MP = 32


def draw_queries(key, part):
    key = jax.random.fold_in(key, 5)
    values = jnp.clip(2.5 * jax.random.normal(key, (TRACT, HEADS, HEAD_DIM), jnp.float32), -12.0, 12.0)
    return values.reshape(TRACT, HEADS * HEAD_DIM).astype(jnp.bfloat16)


def draw_cache_kv(key, part):
    key = jax.random.fold_in(key, 7)
    values = jnp.clip(jax.random.normal(key, (2, CACHE, KV_HEADS, HEAD_DIM), jnp.float32), -6.0, 6.0)
    return values.reshape(2, CACHE, KV_HEADS * HEAD_DIM).astype(jnp.bfloat16)


def draw_image_spans(key, part):
    key = jax.random.fold_in(key, 9)
    first_key, second_key = jax.random.split(key)
    region = TRACT // SPANS
    offsets = jax.random.randint(first_key, (SPANS,), 0, max(region // 4, 1))
    offsets = offsets.at[0].set(0)
    lengths = jax.random.randint(second_key, (SPANS,), max(region // 3, 1), max(3 * region // 4, 2))
    starts = jnp.arange(SPANS, dtype=jnp.int32) * region + offsets
    ends = (starts + lengths).at[SPANS - 1].set(TRACT)
    return jnp.stack([starts, ends], axis=1).astype(jnp.int32)


def block_levels(own_key, shape, cuts, smallest, top_value):
    factor_of, own = 1.0, jax.random.fold_in(own_key, 6)
    for axis_at, parts in cuts:
        draws = jnp.exp(jax.random.uniform(jax.random.fold_in(own, axis_at), (parts,), jnp.float32, smallest / len(cuts), top_value / len(cuts)))
        factor_of = factor_of * jnp.repeat(draws, shape[axis_at] // parts).reshape([-1 if axis == axis_at else 1 for axis in range(len(shape))])
    return factor_of


def routed_block(own_key, own, number, rows, number_of, top, bound, skew):
    ranking = jax.random.permutation(own_key, number_of)
    crowded, ordinary = load_shares(number_of, rows * top, bound, skew, True), load_shares(number_of, rows * top, bound, skew, False)
    places = jnp.arange(number_of)

    def named(sizes, offset_by):
        used = int((sizes > 0).sum())
        fixed = max(1, used // 4)
        passed = fixed + (places - fixed + offset_by * (used - fixed)) % max(1, number_of - fixed)
        return jnp.zeros((number_of,), jnp.int32).at[ranking[jnp.where(places < fixed, places, passed)]].set(jnp.asarray(sizes, jnp.int32))

    sizes = jnp.where(number % 4 == 0, named(crowded, number // 4), named(ordinary, number - number // 4 - 1))
    mixed = jax.random.permutation(jax.random.fold_in(own, 3), number_of)
    giver, receiver = mixed[0:number_of // 2 * 2:2], mixed[1:number_of // 2 * 2:2]
    slack = jnp.minimum(sizes[giver] - 1, bound - sizes[receiver]) // 2
    slack = jnp.where((giver == ranking[0]) | (receiver == ranking[0]) | (sizes[receiver] == 0), 0, jnp.maximum(slack, 0))
    passed = jax.random.randint(jax.random.fold_in(own, 4), (number_of // 2,), 0, 1 << 20) % (slack + 1)
    sizes = sizes.at[giver].add(-passed).at[receiver].add(passed)
    members = jnp.searchsorted(jnp.cumsum(sizes), jnp.arange(rows * top), side="right").astype(jnp.int32)
    grid = members.reshape(top, rows).T
    grid = grid[jax.random.permutation(jax.random.fold_in(own, 1), rows)]
    offset_by = jax.random.randint(jax.random.fold_in(own, 2), (rows, 1), 0, top)
    return jnp.take_along_axis(grid, (jnp.arange(top)[None, :] + offset_by) % top, axis=1)


def load_shares(amount, total, most, slope, full):
    portions = [(1 << 20) // math.isqrt(standing ** slope) + 1 for standing in range(1, amount + 1)]
    largest = most if full else min(most, max(-(-total // amount), total * portions[0] // sum(portions)))
    least = 1 if total - largest >= amount - 1 else 0
    counts, spare = [largest] + [least] * (amount - 1), total - largest - least * (amount - 1)
    while spare > 0:
        free = [i for i in range(1, amount) if counts[i] < largest] or [i for i in range(1, amount) if counts[i] < most]
        pool, remaining = sum([portions[i] for i in free]), spare
        for i in free:
            extra = min(most - counts[i], max(1, remaining * portions[i] // pool), spare)
            counts[i] = counts[i] + extra
            spare = spare - extra
    return np.array(counts)


def scatter_about(stream_key, shape, deviation, most, shards=(), kind=jnp.bfloat16):
    values = jax.random.normal(stream_key, shape, jnp.float32) * deviation
    if len(shards) > 0:
        values = block_levels(stream_key, shape, shards, -0.22, 0.18) * values
    return jnp.clip(values, min=-most, max=most).astype(kind)


def setup_inputs(seed: int = 0) -> dict:
    streams_of = jax.random.split(jax.random.key(seed), 13)
    queries = draw_queries(jax.random.fold_in(streams_of[12], 71), 0)
    new_kv = scatter_about(streams_of[1], (2, TRACT, KV_HEADS * HEAD_DIM), 1.0, 6.0, ((1, 4),))
    cache_kv = draw_cache_kv(jax.random.fold_in(streams_of[12], 71), 0)
    cached_len = jax.random.randint(streams_of[3], (1,), CACHE // 2, CACHE + 1).astype(jnp.int32)
    image_spans = draw_image_spans(jax.random.fold_in(streams_of[12], 71), 0)
    residual = scatter_about(streams_of[5], (TRACT, D), 0.5, 4.0, ((0, 128),))
    out_proj = scatter_about(streams_of[6], (HEADS * HEAD_DIM, D), (HEADS * HEAD_DIM) ** -0.5, 0.0625, ((0, 32),))
    norm_gain = jnp.clip(1.0 + 0.1 * jax.random.normal(streams_of[7], (D,), jnp.float32), 0.5, 1.5)
    routes_keys = jax.random.split(jax.random.fold_in(streams_of[8], 1), TRACT // TOK_MOE)
    routes_turns = jax.random.permutation(jax.random.fold_in(streams_of[8], 3), TRACT // TOK_MOE)
    routes = jax.vmap(lambda own, number: routed_block(jax.random.fold_in(streams_of[8], 2), own, number, TOK_MOE, EXPERTS, TOP, CAP, 2))(routes_keys, routes_turns).reshape((TRACT, TOP))
    gate_weights = jnp.clip(jnp.exp(math.log(1.0) - 2.9957323 * jax.random.uniform(streams_of[9], (TRACT, TOP), jnp.float32) ** block_levels(streams_of[9], (TRACT, TOP), ((0, 128),), -0.2, 0.2)), 0.05, 1.0)
    w_in = scatter_about(streams_of[10], (EXPERTS, D, 2, FF), D ** -0.5, 0.09375, ((0, 32), (3, 4)))
    w_out = scatter_about(streams_of[11], (EXPERTS, FF, D), FF ** -0.5, 0.15625, ((0, 32), (1, 4)))
    return {"queries": queries, "new_kv": new_kv, "cache_kv": cache_kv, "cached_len": cached_len, "image_spans": image_spans, "residual": residual, "out_proj": out_proj, "norm_gain": norm_gain, "routes": routes, "gate_weights": gate_weights, "w_in": w_in, "w_out": w_out}


def span_lookup(image_spans, positions):
    inside = (positions[:, None] >= image_spans[None, :, 0]) & (positions[:, None] < image_spans[None, :, 1])
    labels = jnp.arange(image_spans.shape[0], dtype=jnp.int32)
    return lax.optimization_barrier(jnp.max(jnp.where(inside, labels[None, :], jnp.int32(-1)), axis=1)).astype(jnp.int32)

def reference(queries, new_kv, cache_kv, cached_len, image_spans, residual, out_proj, norm_gain, routes, gate_weights, w_in, w_out):
    group_size = HEADS // KV_HEADS
    key_rows = jnp.concatenate([cache_kv[0], new_kv[0]], axis=0).reshape(CACHE + TRACT, KV_HEADS, HEAD_DIM)
    value_rows = jnp.concatenate([cache_kv[1], new_kv[1]], axis=0).reshape(CACHE + TRACT, KV_HEADS, HEAD_DIM)
    tract_pos = jnp.arange(TRACT, dtype=jnp.int32)
    query_span = span_lookup(image_spans, tract_pos)
    cache_ok = jnp.arange(CACHE, dtype=jnp.int32) < cached_len[0]
    causal = tract_pos[None, :] <= tract_pos[:, None]
    same_span = (query_span[:, None] == query_span[None, :]) & (query_span[:, None] >= 0)
    visible = jnp.concatenate([jnp.broadcast_to(cache_ok[None, :], (TRACT, CACHE)), causal | same_span], axis=1)
    scaling = 1.0 / math.sqrt(HEAD_DIM)
    query_heads = queries.reshape(TRACT, HEADS, HEAD_DIM)

    def one_head(head_index):
        kv_index = head_index // group_size
        query_block = lax.dynamic_index_in_dim(query_heads, head_index, 1, keepdims=False)
        key_block = lax.dynamic_index_in_dim(key_rows, kv_index, 1, keepdims=False)
        value_block = lax.dynamic_index_in_dim(value_rows, kv_index, 1, keepdims=False)
        scores = jnp.dot(query_block, key_block.T, preferred_element_type=jnp.float32) * scaling
        masked = jnp.where(visible, scores, -jnp.inf)
        row_max = lax.optimization_barrier(jnp.max(masked, axis=1, keepdims=True))
        exp_weights = jnp.where(visible, jnp.exp(scores - row_max), jnp.float32(0.0))
        totals = lax.optimization_barrier(jnp.sum(exp_weights, axis=1, keepdims=True))
        mixed_v = jnp.dot(exp_weights.astype(jnp.bfloat16), value_block, preferred_element_type=jnp.float32)
        return (mixed_v / totals).astype(jnp.bfloat16)
    attended = lax.map(one_head, jnp.arange(HEADS, dtype=jnp.int32))
    attended = attended.transpose(1, 0, 2).reshape(TRACT, HEADS * HEAD_DIM)
    groups = attended.reshape(TRACT, N_MP, HEADS_DEV * HEAD_DIM).transpose(1, 0, 2)
    proj_groups = out_proj.reshape(N_MP, HEADS_DEV * HEAD_DIM, D)

    def add_group(running, group_pair):
        partial_value = jnp.dot(group_pair[0], group_pair[1], preferred_element_type=jnp.float32).astype(jnp.bfloat16)
        return (running + lax.optimization_barrier(partial_value).astype(jnp.float32), None)
    projected, _ = lax.scan(add_group, jnp.zeros((TRACT, D), jnp.float32), (groups, proj_groups))
    stream = (residual.astype(jnp.float32) + projected).astype(jnp.bfloat16)
    stream_f = lax.optimization_barrier(stream).astype(jnp.float32)
    normed = (stream_f * lax.rsqrt(lax.optimization_barrier(jnp.mean(stream_f * stream_f, axis=1, keepdims=True)) + 1e-06) * norm_gain).astype(jnp.bfloat16)
    gate_share = gate_weights / lax.optimization_barrier(jnp.sum(gate_weights, axis=1, keepdims=True))
    flat_routes = routes.reshape(-1)
    flat_gates = gate_share.reshape(-1)
    most_rows = N_SEQ * N_MP * CAP

    def one_expert(running, expert):
        chosen = flat_routes == expert
        picked = jnp.nonzero(chosen, size=most_rows, fill_value=0)[0].astype(jnp.int32)
        live_count = jnp.sum(chosen.astype(jnp.int32))
        is_live = jnp.arange(most_rows, dtype=jnp.int32) < live_count
        token_index = (picked // TOP).astype(jnp.int32)
        rows_in = normed[token_index]
        weights_in = lax.dynamic_index_in_dim(w_in, expert, 0, keepdims=False)
        gate_part = jnp.dot(rows_in, weights_in[:, 0, :], preferred_element_type=jnp.float32)
        up_part = jnp.dot(rows_in, weights_in[:, 1, :], preferred_element_type=jnp.float32)
        inner_act = (jax.nn.silu(gate_part) * up_part).astype(jnp.bfloat16)
        weights_out = lax.dynamic_index_in_dim(w_out, expert, 0, keepdims=False)
        grouped = jnp.einsum('rgf,gfd->grd', inner_act.reshape(most_rows, N_SEQ, FF_DEV).astype(jnp.float32), weights_out.reshape(N_SEQ, FF_DEV, D).astype(jnp.float32), precision=lax.Precision.HIGHEST)
        grouped = lax.optimization_barrier(grouped.astype(jnp.bfloat16)).astype(jnp.float32)
        produced = lax.optimization_barrier(jnp.sum(grouped, axis=0))
        scaled = produced * jnp.where(is_live, flat_gates[picked], jnp.float32(0.0))[:, None]
        return (running.at[token_index].add(scaled), None)
    combined, _ = lax.scan(one_expert, jnp.zeros((TRACT, D), jnp.float32), jnp.arange(EXPERTS, dtype=jnp.int32))
    return (stream_f + combined).astype(jnp.bfloat16)
```

```python
import math

import jax
import jax.numpy as jnp
from jax import lax
from jax.experimental import pallas as pl
from jax.experimental.pallas import tpu as pltpu
from jax.sharding import Mesh, PartitionSpec as P

HEAD_DIM = 128
SEQ = ("yh", "core")
MP = ("x", "yl", "z")
NEG = -1e30
BF = jnp.bfloat16
F32 = jnp.float32
ANY_LAST = (((1,), (1,)), ((), ()))


def attn_kernel(info, q_ref, kc_ref, vc_ref, kn_ref, vn_ref, out_ref, s_ref):
    rows = q_ref.shape[0]
    cache_rows = kc_ref.shape[1]
    chunk = kn_ref.shape[1]
    chunks = cache_rows // chunk
    coef = math.log2(math.e) / math.sqrt(HEAD_DIM)
    valid = info[1]
    key_pos = info[2] + lax.broadcasted_iota(jnp.int32, (1, chunk), 1)
    pos = info[3] + lax.broadcasted_iota(jnp.int32, (rows, 1), 0)
    limit = pos
    for a in range(3):
        start, end = info[4 + 2 * a], info[5 + 2 * a]
        limit = jnp.where((pos >= start) & (pos < end), jnp.maximum(limit, end - 1), limit)
    tract_ok = key_pos <= limit
    lane = lax.broadcasted_iota(jnp.int32, (rows, 128), 1)
    stats = jnp.zeros((rows, 128), F32)
    column = lax.broadcasted_iota(jnp.int32, (1, chunk), 1)
    for h in range(2):
        q = q_ref[:, h * HEAD_DIM : (h + 1) * HEAD_DIM]
        top = None
        for c in range(chunks + 1):
            if c < chunks:
                k = kc_ref[0, c * chunk : (c + 1) * chunk, :]
                s = lax.dot_general(q, k, ANY_LAST, preferred_element_type=F32)
                s = s + jnp.where(column < valid - c * chunk, 0.0, NEG)
            else:
                s = lax.dot_general(q, kn_ref[0], ANY_LAST, preferred_element_type=F32)
                s = jnp.where(tract_ok, s, NEG)
            s_ref[h, :, c * chunk : (c + 1) * chunk] = s
            top = s if top is None else jnp.maximum(top, s)
        m = jnp.max(top, axis=1, keepdims=True) * coef
        total = None
        acc = None
        for c in range(chunks + 1):
            p = jnp.exp2(s_ref[h, :, c * chunk : (c + 1) * chunk] * coef - m)
            total = p if total is None else total + p
            v = vc_ref[0, c * chunk : (c + 1) * chunk, :] if c < chunks else vn_ref[0]
            part = jnp.dot(p.astype(BF), v, preferred_element_type=F32)
            acc = part if acc is None else acc + part
        total = jnp.sum(total, axis=1, keepdims=True)
        out_ref[0:rows, h * HEAD_DIM : (h + 1) * HEAD_DIM] = (acc / total).astype(BF)
        level = m + jnp.log2(total)
        for part in range(3):
            piece = level.astype(BF).astype(F32)
            level = level - piece
            stats = jnp.where(lane == 3 * h + part, piece, stats)
    out_ref[rows : rows + 16, :] = stats.T[0:16, :].astype(BF)


def attend(info, q, cache_kv, new_kv):
    rows = q.shape[0]
    cache_rows, new_rows = cache_kv.shape[1], new_kv.shape[1]
    keys = cache_rows + new_rows
    return pl.pallas_call(
        attn_kernel,
        grid_spec=pltpu.PrefetchScalarGridSpec(
            num_scalar_prefetch=1,
            grid=(1,),
            in_specs=[
                pl.BlockSpec((rows, 2 * HEAD_DIM), lambda i, t: (0, 0)),
                pl.BlockSpec((1, cache_rows, HEAD_DIM), lambda i, t: (0, 0, t[0])),
                pl.BlockSpec((1, cache_rows, HEAD_DIM), lambda i, t: (1, 0, t[0])),
                pl.BlockSpec((1, new_rows, HEAD_DIM), lambda i, t: (0, 0, t[0])),
                pl.BlockSpec((1, new_rows, HEAD_DIM), lambda i, t: (1, 0, t[0])),
            ],
            out_specs=pl.BlockSpec((rows + 16, 2 * HEAD_DIM), lambda i, t: (0, 0)),
            scratch_shapes=[pltpu.VMEM((2, rows, keys), F32)],
        ),
        out_shape=jax.ShapeDtypeStruct((rows + 16, 2 * HEAD_DIM), BF),
        compiler_params=pltpu.CompilerParams(vmem_limit_bytes=32 << 20),
        cost_estimate=pl.CostEstimate(
            flops=8 * rows * keys * HEAD_DIM,
            bytes_accessed=4 * keys * HEAD_DIM,
            transcendentals=2 * rows * keys,
        ),
        name="attend",
    )(info, q, cache_kv, cache_kv, new_kv, new_kv)


def merge_kernel(a_ref, b_ref, c_ref, d_ref, out_ref):
    parts = (a_ref, b_ref, c_ref, d_ref)
    rows = out_ref.shape[0]
    pad = jnp.zeros((112, rows), F32)
    stats = [
        jnp.concatenate([p[rows : rows + 16, :].astype(F32), pad], axis=0).T for p in parts
    ]
    for h in range(2):
        cols = slice(h * HEAD_DIM, (h + 1) * HEAD_DIM)
        levels = [
            t[:, 3 * h : 3 * h + 1] + t[:, 3 * h + 1 : 3 * h + 2] + t[:, 3 * h + 2 : 3 * h + 3]
            for t in stats
        ]
        best = jnp.maximum(
            jnp.maximum(levels[0], levels[1]), jnp.maximum(levels[2], levels[3])
        )
        weights = [jnp.exp2(v - best) for v in levels]
        total = weights[0] + weights[1] + weights[2] + weights[3]
        acc = None
        for w, p in zip(weights, parts):
            term = p[0:rows, cols].astype(F32) * w
            acc = term if acc is None else acc + term
        out_ref[:, cols] = (acc / total).astype(BF)


def merge(parts):
    rows = parts[0].shape[0] - 16
    return pl.pallas_call(
        merge_kernel,
        out_shape=jax.ShapeDtypeStruct((rows, 2 * HEAD_DIM), BF),
        cost_estimate=pl.CostEstimate(flops=1 << 20, bytes_accessed=5 << 17, transcendentals=0),
        name="merge",
    )(*parts)


def project_kernel(*refs):
    out_ref = refs[8]
    acc = None
    for a, w in zip(refs[:4], refs[4:8]):
        part = jnp.dot(a[...], w[...], preferred_element_type=F32)
        acc = part if acc is None else acc + part
    out_ref[...] = acc.astype(BF)


def project(parts, weights):
    rows, depth = parts[0].shape
    width = weights[0].shape[1]
    step = 256
    return pl.pallas_call(
        project_kernel,
        grid=(width // step,),
        in_specs=[pl.BlockSpec((rows, depth), lambda i: (0, 0))] * 4
        + [pl.BlockSpec((depth, step), lambda i: (0, i))] * 4,
        out_specs=pl.BlockSpec((rows, step), lambda i: (0, i)),
        out_shape=jax.ShapeDtypeStruct((rows, width), BF),
        cost_estimate=pl.CostEstimate(
            flops=8 * rows * depth * width, bytes_accessed=8 * depth * width, transcendentals=0
        ),
        name="project",
    )(*parts, *weights)


def expert_kernel(
    own_ref, other_ref, gain_ref, win_ref, wout_ref, kept_ref, sent_ref, x_ref, hidden_ref
):
    step = pl.program_id(0)
    groups, chunks, _, chunk = own_ref.shape
    half = groups * 8
    ff = wout_ref.shape[1]
    width = chunks * chunk

    @pl.when(step == 0)
    def _():
        for side, ref in enumerate((own_ref, other_ref)):

            @pl.loop(0, groups // 2)
            def _(pair):
                normed = []
                for j in range(2):
                    v = [ref[2 * pair + j, z].astype(F32) for z in range(chunks)]
                    square = v[0] * v[0]
                    for z in range(1, chunks):
                        square = square + v[z] * v[z]
                    scale = lax.rsqrt(
                        jnp.sum(square, axis=1, keepdims=True) * (1.0 / width) + 1e-6
                    )
                    normed.append([v[z] * scale * gain_ref[z : z + 1, :] for z in range(chunks)])
                at = pl.multiple_of(side * half + pair * 16, 16)
                for e in range(2):
                    for z in range(chunks):
                        x_ref[e, z, pl.ds(at, 16), :] = jnp.concatenate(
                            [normed[j][z][8 * e : 8 * e + 8] for j in range(2)], axis=0
                        ).astype(BF)

    @pl.when(step < 2 * chunks)
    def _():
        e, z = step // chunks, step % chunks
        part = jnp.dot(x_ref[e, z], win_ref[0], preferred_element_type=F32)

        @pl.when(z == 0)
        def _():
            hidden_ref[e] = part

        @pl.when(z > 0)
        def _():
            hidden_ref[e] = hidden_ref[e] + part

    @pl.when(step >= 2 * chunks)
    def _():
        produced = []
        for e in range(2):
            gate, up = hidden_ref[e, :, :ff], hidden_ref[e, :, ff:]
            act = (gate / (1.0 + jnp.exp(-gate)) * up).astype(BF)
            produced.append(jnp.dot(act, wout_ref[e], preferred_element_type=F32))
        for side, ref in enumerate((kept_ref, sent_ref)):
            both = [
                p[side * half : (side + 1) * half].reshape(groups, 8, chunk) for p in produced
            ]
            ref[:, 0] = jnp.concatenate(both, axis=1).astype(BF)


def experts(own, other, gain, w_in, w_out):
    groups, chunks, _, chunk = own.shape
    ff = w_out.shape[1]
    last = 2 * chunks - 1
    shape = jax.ShapeDtypeStruct(own.shape, BF)
    rows = 2 * groups * 8

    def out_map(i):
        return (0, jnp.maximum(i - last - 1, 0), 0, 0)

    return pl.pallas_call(
        expert_kernel,
        grid=(3 * chunks,),
        in_specs=[
            pl.BlockSpec(own.shape, lambda i: (0, 0, 0, 0)),
            pl.BlockSpec(own.shape, lambda i: (0, 0, 0, 0)),
            pl.BlockSpec((chunks, chunk), lambda i: (0, 0)),
            pl.BlockSpec(
                (1, chunk, 2 * ff),
                lambda i: (jnp.minimum(i, last) // chunks, jnp.minimum(i, last) % chunks, 0),
            ),
            pl.BlockSpec((2, ff, chunk), lambda i: (0, 0, jnp.maximum(i - last - 1, 0))),
        ],
        out_specs=[
            pl.BlockSpec((groups, 1, 16, chunk), out_map),
            pl.BlockSpec((groups, 1, 16, chunk), out_map),
        ],
        out_shape=[shape, shape],
        scratch_shapes=[
            pltpu.VMEM((2, chunks, rows, chunk), BF),
            pltpu.VMEM((2, rows, 2 * ff), F32),
        ],
        compiler_params=pltpu.CompilerParams(vmem_limit_bytes=48 << 20),
        cost_estimate=pl.CostEstimate(
            flops=12 * rows * chunks * chunk * ff,
            bytes_accessed=12 * chunks * chunk * ff,
            transcendentals=2 * rows * ff,
        ),
        name="experts",
    )(own, other, gain.reshape(chunks, chunk), w_in, w_out)


def swap(v, axes, bit):
    count = 4 if len(axes) == 2 else 2
    return lax.ppermute(v, axes, [(i, i ^ bit) for i in range(count)])


def shift(v, d):
    return lax.ppermute(v, "z", [(i, (i + d) % 4) for i in range(4)])


def local(
    queries,
    new_kv,
    cache_kv,
    cached_len,
    image_spans,
    residual,
    out_proj,
    norm_gain,
    routes,
    gate_weights,
    w_in,
    w_out,
):
    seq = lax.axis_index(SEQ)
    z_at = lax.axis_index("z")
    tract = queries.shape[0]
    cache = cache_kv.shape[1]
    tok = residual.shape[0]
    width = residual.shape[1]
    quarter = width // 4

    query_parts = [queries] + [swap(queries, SEQ, d) for d in (1, 2, 3)]

    def column_block(z):
        return lax.dynamic_slice_in_dim(out_proj, (z % 4) * quarter, quarter, 1)

    proj_parts = [column_block(z_at)] + [shift(column_block(z_at + d), d) for d in (1, 2, 3)]

    residual_part = lax.all_to_all(
        residual.reshape(tok, 4, quarter).transpose(1, 0, 2),
        "z",
        split_axis=0,
        concat_axis=0,
        tiled=True,
    ).reshape(4 * tok, quarter)

    gate_share = gate_weights / jnp.sum(gate_weights, axis=1, keepdims=True)
    top = routes.shape[1]
    table = lax.all_gather(
        jnp.concatenate([routes.astype(F32), gate_share], axis=1), "z", axis=0, tiled=True
    )
    named = table[:, :top].astype(jnp.int32).reshape(4, tok, top)
    shares = table[:, top:]
    same = named[:, :, :, None, None] == named[:, None, None, :, :]
    earlier = (
        jnp.arange(tok)[:, None] > jnp.arange(tok)[None, :]
    )[None, :, None, :, None]
    rank = jnp.sum((same & earlier).astype(jnp.int32), axis=(3, 4))
    block = jnp.arange(4, dtype=jnp.int32)[:, None, None]
    slot = ((named // 2) * 16 + (named % 2) * 8 + block * 2 + rank).reshape(4 * tok, top)
    slots = 32 * 16
    placement = slot[:, :, None] == jnp.arange(slots, dtype=jnp.int32)[None, None, :]
    selector = jnp.sum(placement.astype(F32), axis=1).astype(BF)
    combiner = jnp.sum(jnp.where(placement, shares[:, :, None], 0.0), axis=1)
    coarse = combiner.astype(BF)
    fine = (combiner - coarse.astype(F32)).astype(BF)

    valid = jnp.clip(cached_len[0] - seq * cache, 0, cache)
    answers = []
    for d in range(4):
        info = jnp.concatenate(
            [
                jnp.stack(
                    [lax.axis_index("x"), valid, seq * tract, (seq ^ d) * tract]
                ).astype(jnp.int32),
                image_spans.reshape(-1),
            ]
        )
        part = attend(info, query_parts[d], cache_kv, new_kv)
        answers.append(swap(part, SEQ, d) if d else part)
    attended = merge(answers)

    head_parts = [attended] + [shift(attended, d) for d in (1, 2, 3)]
    partial = project(head_parts, proj_parts)
    arrived = lax.all_to_all(
        partial.reshape(8, 4 * tok, quarter), ("x", "yl"), split_axis=0, concat_axis=0, tiled=True
    )
    stream = (
        residual_part.astype(F32) + jnp.sum(arrived.astype(F32), axis=0)
    ).astype(BF)

    twice = jnp.concatenate([selector, selector], axis=1)
    outgoing = lax.dot_general(
        twice, stream, (((0,), (0,)), ((), ())), preferred_element_type=F32
    ).astype(BF)
    own = lax.all_to_all(
        outgoing.reshape(64, 16, quarter), ("yh",) + MP, split_axis=0, concat_axis=0, tiled=True
    )
    other = swap(own, ("core",), 1)
    shaped = (16, 4, 16, quarter)
    joined = w_in.reshape(w_in.shape[0], w_in.shape[1], 2 * w_in.shape[3])
    kept, sent = experts(own.reshape(shaped), other.reshape(shaped), norm_gain, joined, w_out)
    got = swap(sent, ("core",), 1)
    summed = (kept.astype(F32) + got.astype(F32)).astype(BF)
    returned = lax.all_to_all(
        summed.reshape(64, 16, quarter), ("yh",) + MP, split_axis=0, concat_axis=0, tiled=True
    ).reshape(2 * slots, quarter)

    combined = jnp.dot(
        jnp.concatenate([coarse, coarse], axis=1), returned, preferred_element_type=F32
    ) + jnp.dot(jnp.concatenate([fine, fine], axis=1), returned, preferred_element_type=F32)
    mixed = (stream.astype(F32) + combined).astype(BF)
    return (
        lax.all_to_all(
            mixed.reshape(4, tok, quarter), "z", split_axis=0, concat_axis=0, tiled=True
        )
        .transpose(1, 0, 2)
        .reshape(tok, width)
    )


def solution(mesh):
    fine = Mesh(mesh.devices.reshape(2, 2, 4, 2, 4), SEQ + MP)
    in_specs = (
        P(SEQ, MP),
        P(None, SEQ, None),
        P(None, SEQ, None),
        P(),
        P(),
        P(SEQ + MP, None),
        P(MP, None),
        P(),
        P(SEQ + MP, None),
        P(SEQ + MP, None),
        P(MP, None, None, SEQ),
        P(MP, SEQ, None),
    )
    return jax.shard_map(
        local, mesh=fine, in_specs=in_specs, out_specs=P(SEQ + MP, None), check_vma=False
    )
```

```python
import math

import jax
import jax.numpy as jnp
from jax import lax
from jax.experimental import pallas as pl
from jax.experimental.pallas import tpu as pltpu
from jax.sharding import Mesh, PartitionSpec as P

HEAD_DIM = 128
SEQ = ("yh", "core")
MP = ("x", "yl", "z")
NEG = -1e30
BF = jnp.bfloat16
F32 = jnp.float32
ANY_LAST = (((1,), (1,)), ((), ()))


def attn_kernel(info, qa_ref, qb_ref, kc_ref, vc_ref, kn_ref, vn_ref, oa_ref, ob_ref, s_ref):
    rows = qa_ref.shape[0]
    cache_rows = kc_ref.shape[1]
    chunk = kn_ref.shape[1]
    chunks = cache_rows // chunk
    coef = math.log2(math.e) / math.sqrt(HEAD_DIM)
    valid = info[1]
    key_pos = info[2] + lax.broadcasted_iota(jnp.int32, (1, chunk), 1)
    lane = lax.broadcasted_iota(jnp.int32, (rows, 128), 1)
    column = lax.broadcasted_iota(jnp.int32, (1, chunk), 1)
    for b, (q_ref, out_ref) in enumerate(((qa_ref, oa_ref), (qb_ref, ob_ref))):
        pos = info[3 + b] + lax.broadcasted_iota(jnp.int32, (rows, 1), 0)
        limit = pos
        for a in range(3):
            start, end = info[5 + 2 * a], info[6 + 2 * a]
            limit = jnp.where((pos >= start) & (pos < end), jnp.maximum(limit, end - 1), limit)
        tract_ok = key_pos <= limit
        stats = jnp.zeros((rows, 128), F32)
        for h in range(2):
            at = 2 * b + h
            q = q_ref[:, h * HEAD_DIM : (h + 1) * HEAD_DIM]
            top = None
            for c in range(chunks + 1):
                if c < chunks:
                    k = kc_ref[0, c * chunk : (c + 1) * chunk, :]
                    s = lax.dot_general(q, k, ANY_LAST, preferred_element_type=F32)
                    s = s + jnp.where(column < valid - c * chunk, 0.0, NEG)
                else:
                    s = lax.dot_general(q, kn_ref[0], ANY_LAST, preferred_element_type=F32)
                    s = jnp.where(tract_ok, s, NEG)
                s_ref[at, :, c * chunk : (c + 1) * chunk] = s
                top = s if top is None else jnp.maximum(top, s)
            m = jnp.max(top, axis=1, keepdims=True) * coef
            total = None
            acc = None
            for c in range(chunks + 1):
                p = jnp.exp2(s_ref[at, :, c * chunk : (c + 1) * chunk] * coef - m)
                total = p if total is None else total + p
                v = vc_ref[0, c * chunk : (c + 1) * chunk, :] if c < chunks else vn_ref[0]
                part = jnp.dot(p.astype(BF), v, preferred_element_type=F32)
                acc = part if acc is None else acc + part
            total = jnp.sum(total, axis=1, keepdims=True)
            out_ref[0:rows, h * HEAD_DIM : (h + 1) * HEAD_DIM] = (acc / total).astype(BF)
            level = m + jnp.log2(total)
            for part in range(3):
                piece = level.astype(BF).astype(F32)
                level = level - piece
                stats = jnp.where(lane == 3 * h + part, piece, stats)
        out_ref[rows : rows + 16, :] = stats.T[0:16, :].astype(BF)


def attend(info, qa, qb, cache_kv, new_kv):
    rows = qa.shape[0]
    cache_rows, new_rows = cache_kv.shape[1], new_kv.shape[1]
    keys = cache_rows + new_rows
    whole = pl.BlockSpec((rows, 2 * HEAD_DIM), lambda i, t: (0, 0))
    result = pl.BlockSpec((rows + 16, 2 * HEAD_DIM), lambda i, t: (0, 0))
    shape = jax.ShapeDtypeStruct((rows + 16, 2 * HEAD_DIM), BF)
    return pl.pallas_call(
        attn_kernel,
        grid_spec=pltpu.PrefetchScalarGridSpec(
            num_scalar_prefetch=1,
            grid=(1,),
            in_specs=[
                whole,
                whole,
                pl.BlockSpec((1, cache_rows, HEAD_DIM), lambda i, t: (0, 0, t[0])),
                pl.BlockSpec((1, cache_rows, HEAD_DIM), lambda i, t: (1, 0, t[0])),
                pl.BlockSpec((1, new_rows, HEAD_DIM), lambda i, t: (0, 0, t[0])),
                pl.BlockSpec((1, new_rows, HEAD_DIM), lambda i, t: (1, 0, t[0])),
            ],
            out_specs=[result, result],
            scratch_shapes=[pltpu.VMEM((4, rows, keys), F32)],
        ),
        out_shape=[shape, shape],
        compiler_params=pltpu.CompilerParams(vmem_limit_bytes=32 << 20),
        cost_estimate=pl.CostEstimate(
            flops=32 * rows * keys * HEAD_DIM,
            bytes_accessed=4 * keys * HEAD_DIM,
            transcendentals=4 * rows * keys,
        ),
        name="attend",
    )(info, qa, qb, cache_kv, cache_kv, new_kv, new_kv)


def project_kernel(a_ref, b_ref, c_ref, d_ref, w_ref, out_ref, att_ref):
    parts = (a_ref, b_ref, c_ref, d_ref)
    rows = out_ref.shape[0]

    @pl.when(pl.program_id(0) == 0)
    def _():
        pad = jnp.zeros((112, rows), F32)
        stats = [
            jnp.concatenate([p[rows : rows + 16, :].astype(F32), pad], axis=0).T for p in parts
        ]
        for h in range(2):
            cols = slice(h * HEAD_DIM, (h + 1) * HEAD_DIM)
            at = 3 * h
            levels = [
                t[:, at : at + 1] + t[:, at + 1 : at + 2] + t[:, at + 2 : at + 3] for t in stats
            ]
            best = jnp.maximum(
                jnp.maximum(levels[0], levels[1]), jnp.maximum(levels[2], levels[3])
            )
            weights = [jnp.exp2(v - best) for v in levels]
            total = weights[0] + weights[1] + weights[2] + weights[3]
            acc = None
            for w, p in zip(weights, parts):
                term = p[0:rows, cols].astype(F32) * w
                acc = term if acc is None else acc + term
            att_ref[:, cols] = (acc / total).astype(BF)

    out_ref[...] = jnp.dot(att_ref[...], w_ref[...], preferred_element_type=F32).astype(BF)


def project(parts, out_proj):
    rows, depth = parts[0].shape[0] - 16, parts[0].shape[1]
    width = out_proj.shape[1]
    step = 1024
    return pl.pallas_call(
        project_kernel,
        grid=(width // step,),
        in_specs=[pl.BlockSpec((rows + 16, depth), lambda i: (0, 0))] * 4
        + [pl.BlockSpec((depth, step), lambda i: (0, i))],
        out_specs=pl.BlockSpec((rows, step), lambda i: (0, i)),
        out_shape=jax.ShapeDtypeStruct((rows, width), BF),
        scratch_shapes=[pltpu.VMEM((rows, depth), BF)],
        cost_estimate=pl.CostEstimate(
            flops=2 * rows * depth * width, bytes_accessed=4 * depth * width, transcendentals=0
        ),
        name="project",
    )(*parts, out_proj)


def settle_kernel(arrived_ref, residual_ref, gain_ref, pick_ref, stream_ref, out_ref):
    tok, width = residual_ref.shape
    groups = arrived_ref.shape[0]
    chunk = out_ref.shape[2]
    chunks = width // chunk
    pieces = []
    square = None
    for c in range(chunks):
        cols = slice(c * chunk, (c + 1) * chunk)
        acc = arrived_ref[0, :, cols].astype(F32)
        for g in range(1, groups):
            acc = acc + arrived_ref[g, :, cols].astype(F32)
        stream = (residual_ref[:, cols].astype(F32) + acc).astype(BF)
        stream_ref[:, cols] = stream
        piece = stream.astype(F32)
        pieces.append(piece)
        term = jnp.sum(piece * piece, axis=1, keepdims=True)
        square = term if square is None else square + term
    scale = lax.rsqrt(square * (1.0 / width) + 1e-6)
    normed = [
        p * scale * gain_ref[:, c * chunk : (c + 1) * chunk] for c, p in enumerate(pieces)
    ]
    stacked = jnp.concatenate(normed, axis=0).astype(BF)
    rows = jnp.dot(pick_ref[...], stacked, preferred_element_type=F32).astype(BF)
    half = out_ref.shape[0] // 2
    rows = rows.reshape(half, 16, chunk)
    out_ref[0:half] = rows
    out_ref[half : 2 * half] = rows


def settle(arrived, residual, gain, pick):
    tok, width = residual.shape
    chunk = width // 4
    return pl.pallas_call(
        settle_kernel,
        out_shape=[
            jax.ShapeDtypeStruct((tok, width), BF),
            jax.ShapeDtypeStruct((pick.shape[0] // 8, 16, chunk), BF),
        ],
        compiler_params=pltpu.CompilerParams(vmem_limit_bytes=32 << 20),
        cost_estimate=pl.CostEstimate(
            flops=1 << 26, bytes_accessed=4 << 20, transcendentals=0
        ),
        name="settle",
    )(arrived, residual, gain.reshape(1, width), pick)


def expert_kernel(
    own_ref, other_ref, perm_ref, back_ref, win_ref, wout_ref, kept_ref, sent_ref, x_ref,
    hidden_ref, z_ref
):
    step = pl.program_id(0)
    chunk = own_ref.shape[2]
    chunks = 4
    sources = own_ref.shape[0]
    half = sources * 2
    ff = wout_ref.shape[1]
    sides = ((own_ref, kept_ref), (other_ref, sent_ref))

    @pl.when(step == 0)
    def _():
        for side, (ref, _) in enumerate(sides):
            for g in range(sources // 16):
                block = ref[16 * g : 16 * g + 16].reshape(256, chunk)
                y = jnp.dot(perm_ref[...], block, preferred_element_type=F32).astype(BF)
                at = side * half + g * 32
                for e in range(2):
                    for c in range(chunks):
                        first = (e * chunks + c) * 32
                        x_ref[e, c, at : at + 32, :] = y[first : first + 32]

    @pl.when(step < chunks)
    def _():
        for e in range(2):
            for p in range(2):
                cols = slice(p * ff, (p + 1) * ff)
                part = jnp.dot(x_ref[e, step], win_ref[e, p], preferred_element_type=F32)

                @pl.when(step == 0)
                def _():
                    hidden_ref[e, :, cols] = part

                @pl.when(step > 0)
                def _():
                    hidden_ref[e, :, cols] = hidden_ref[e, :, cols] + part

    @pl.when(step >= chunks)
    def _():
        c = step - chunks
        for e in range(2):
            gate, up = hidden_ref[e, :, :ff], hidden_ref[e, :, ff:]
            act = (gate / (1.0 + jnp.exp(-gate)) * up).astype(BF)
            z_ref[e, c] = jnp.dot(act, wout_ref[e], preferred_element_type=F32).astype(BF)

    @pl.when(step == 2 * chunks - 1)
    def _():
        for side, (_, ref) in enumerate(sides):
            for g in range(sources // 16):
                at = side * half + g * 32
                block = jnp.concatenate(
                    [z_ref[e, c, at : at + 32, :] for e in range(2) for c in range(chunks)],
                    axis=0,
                )
                y = jnp.dot(back_ref[...], block, preferred_element_type=F32).astype(BF)
                ref[16 * g : 16 * g + 16] = y.reshape(16, 16, chunk)


def experts(own, other, perm, w_in, w_out):
    sources, _, chunk = own.shape
    chunks = 4
    ff = w_out.shape[1]
    rows = 4 * sources
    shape = jax.ShapeDtypeStruct(own.shape, BF)
    whole = pl.BlockSpec(own.shape, lambda i: (0, 0, 0))
    square = pl.BlockSpec(perm.shape, lambda i: (0, 0))
    return pl.pallas_call(
        expert_kernel,
        grid=(2 * chunks,),
        in_specs=[
            whole,
            whole,
            square,
            square,
            pl.BlockSpec((2, 2, chunk, ff), lambda i: (0, 0, jnp.minimum(i, chunks - 1), 0)),
            pl.BlockSpec((2, ff, chunk), lambda i: (0, 0, jnp.maximum(i - chunks, 0))),
        ],
        out_specs=[whole, whole],
        out_shape=[shape, shape],
        scratch_shapes=[
            pltpu.VMEM((2, chunks, rows, chunk), BF),
            pltpu.VMEM((2, rows, 2 * ff), F32),
            pltpu.VMEM((2, chunks, rows, chunk), BF),
        ],
        compiler_params=pltpu.CompilerParams(vmem_limit_bytes=56 << 20),
        cost_estimate=pl.CostEstimate(
            flops=12 * rows * chunks * chunk * ff,
            bytes_accessed=12 * chunks * chunk * ff,
            transcendentals=2 * rows * ff,
        ),
        name="experts",
    )(own, other, perm, perm.T, w_in, w_out)


def combine_kernel(share_ref, returned_ref, stream_ref, out_ref):
    tok = stream_ref.shape[0]
    chunk = returned_ref.shape[1]
    both = jnp.dot(share_ref[...], returned_ref[...], preferred_element_type=F32)
    half = both.shape[0] // 2
    total = both[:half] + both[half:]
    for c in range(half // tok):
        cols = slice(c * chunk, (c + 1) * chunk)
        out_ref[:, cols] = (
            stream_ref[:, cols].astype(F32) + total[c * tok : (c + 1) * tok]
        ).astype(BF)


def combine(share, returned, stream):
    return pl.pallas_call(
        combine_kernel,
        out_shape=jax.ShapeDtypeStruct(stream.shape, BF),
        compiler_params=pltpu.CompilerParams(vmem_limit_bytes=32 << 20),
        name="combine",
    )(share, returned, stream)


def swap(v, axes, bit):
    count = 4 if len(axes) == 2 else 2
    return lax.ppermute(v, axes, [(i, i ^ bit) for i in range(count)])


def local(
    queries,
    new_kv,
    cache_kv,
    cached_len,
    image_spans,
    residual,
    out_proj,
    norm_gain,
    routes,
    gate_weights,
    w_in,
    w_out,
):
    seq = lax.axis_index(SEQ)
    tract = queries.shape[0]
    cache = cache_kv.shape[1]
    tok = residual.shape[0]
    width = residual.shape[1]
    quarter = width // 4
    spread = ("yh",) + MP

    query_parts = [queries] + [swap(queries, SEQ, d) for d in (1, 2, 3)]
    valid = jnp.clip(cached_len[0] - seq * cache, 0, cache)

    def attend_pair(d):
        info = jnp.concatenate(
            [
                jnp.stack(
                    [
                        lax.axis_index("x"),
                        valid,
                        seq * tract,
                        (seq ^ d) * tract,
                        (seq ^ (d + 1)) * tract,
                    ]
                ).astype(jnp.int32),
                image_spans.reshape(-1),
            ]
        )
        return attend(info, query_parts[d], query_parts[d + 1], cache_kv, new_kv)

    mine, beside = attend_pair(0)
    across, diagonal = attend_pair(2)
    parts = [mine, swap(beside, SEQ, 1), swap(across, SEQ, 2), swap(diagonal, SEQ, 3)]
    partial = project(parts, out_proj)
    arrived = lax.all_to_all(
        partial.reshape(32, tok, width), MP, split_axis=0, concat_axis=0, tiled=True
    )

    gate_share = gate_weights / jnp.sum(gate_weights, axis=1, keepdims=True)
    top = routes.shape[1]
    same = routes[:, :, None, None] == routes[None, None, :, :]
    earlier = jnp.arange(tok)[:, None] > jnp.arange(tok)[None, :]
    rank = jnp.sum((same & earlier[:, None, :, None]).astype(jnp.int32), axis=(2, 3))
    slot = routes * 2 + rank
    pairs = 32
    placement = slot[:, :, None] == jnp.arange(pairs * 4, dtype=jnp.int32)[None, None, :]
    chosen = jnp.sum(placement.astype(F32), axis=1)
    weighed = jnp.sum(jnp.where(placement, gate_share[:, :, None], 0.0), axis=1)
    eye = jnp.eye(4, dtype=F32)

    def spread_rows(v):
        wide = v.reshape(1, tok, pairs, 1, 4) * eye.reshape(4, 1, 1, 4, 1)
        return wide.reshape(4 * tok, pairs * 16)

    pick = spread_rows(chosen).astype(BF).T
    share = spread_rows(weighed)
    coarse = share.astype(BF)
    fine = (share - coarse.astype(F32)).astype(BF)
    share = jnp.concatenate([coarse, fine], axis=0)
    share = jnp.concatenate([share, share], axis=1)

    perm = jnp.eye(256, dtype=BF).reshape(16, 4, 2, 2, 256).transpose(2, 1, 0, 3, 4)
    perm = perm.reshape(256, 256)

    stream, outgoing = settle(arrived, residual, norm_gain, pick)

    outgoing, held = lax.optimization_barrier((outgoing, w_in))
    own = lax.all_to_all(outgoing, spread, split_axis=0, concat_axis=0, tiled=True)
    turned = held.transpose(0, 2, 1, 3)
    own, turned = lax.optimization_barrier((own, turned))
    other = swap(own, ("core",), 1)
    kept, sent = experts(own, other, perm, turned, w_out)
    got = swap(sent, ("core",), 1)
    summed = (kept.astype(F32) + got.astype(F32)).astype(BF)
    returned = lax.all_to_all(summed, spread, split_axis=0, concat_axis=0, tiled=True)
    return combine(share, returned.reshape(-1, quarter), stream)


def solution(mesh):
    fine = Mesh(mesh.devices.reshape(2, 2, 4, 2, 4), SEQ + MP)
    in_specs = (
        P(SEQ, MP),
        P(None, SEQ, None),
        P(None, SEQ, None),
        P(),
        P(),
        P(SEQ + MP, None),
        P(MP, None),
        P(),
        P(SEQ + MP, None),
        P(SEQ + MP, None),
        P(MP, None, None, SEQ),
        P(MP, SEQ, None),
    )
    return jax.shard_map(
        local, mesh=fine, in_specs=in_specs, out_specs=P(SEQ + MP, None), check_vma=False
    )
```

```python
import functools
import math

import jax
import jax.numpy as jnp
import numpy as np
from jax import lax
from jax.experimental import pallas as pl
from jax.experimental.pallas import tpu as pltpu
from jax.sharding import Mesh, PartitionSpec as P

HEAD_DIM = 128
SEQ = ("yh", "core")
MP = ("x", "yl", "z")
NEG = -1e30
BF = jnp.bfloat16
F32 = jnp.float32
ANY_LAST = (((1,), (1,)), ((), ()))


def attn_kernel(first, info, qa_ref, qb_ref, kc_ref, vc_ref, kn_ref, vn_ref, oa_ref, ob_ref, s_ref):
    rows = qa_ref.shape[0]
    cache_rows = kc_ref.shape[1]
    chunk = kn_ref.shape[1]
    chunks = cache_rows // chunk
    coef = math.log2(math.e) / math.sqrt(HEAD_DIM)
    valid = info[1]
    key_pos = info[2] * rows + lax.broadcasted_iota(jnp.int32, (1, chunk), 1)
    lane = lax.broadcasted_iota(jnp.int32, (rows, 128), 1)
    column = lax.broadcasted_iota(jnp.int32, (1, chunk), 1)
    for b, (q_ref, out_ref) in enumerate(((qa_ref, oa_ref), (qb_ref, ob_ref))):
        pos = (info[2] ^ (first + b)) * rows + lax.broadcasted_iota(jnp.int32, (rows, 1), 0)
        limit = pos
        for a in range(3):
            start, end = info[3 + 2 * a], info[4 + 2 * a]
            limit = jnp.where((pos >= start) & (pos < end), jnp.maximum(limit, end - 1), limit)
        tract_ok = key_pos <= limit
        stats = jnp.zeros((rows, 128), F32)
        for h in range(2):
            at = 2 * b + h
            q = q_ref[:, h * HEAD_DIM : (h + 1) * HEAD_DIM]
            top = None
            for c in range(chunks + 1):
                if c < chunks:
                    k = kc_ref[0, c * chunk : (c + 1) * chunk, :]
                    s = lax.dot_general(q, k, ANY_LAST, preferred_element_type=F32)
                    s = s + jnp.where(column < valid - c * chunk, 0.0, NEG)
                else:
                    s = lax.dot_general(q, kn_ref[0], ANY_LAST, preferred_element_type=F32)
                    s = jnp.where(tract_ok, s, NEG)
                s_ref[at, :, c * chunk : (c + 1) * chunk] = s
                top = s if top is None else jnp.maximum(top, s)
            m = jnp.max(top, axis=1, keepdims=True) * coef
            total = None
            acc = None
            for c in range(chunks + 1):
                p = jnp.exp2(s_ref[at, :, c * chunk : (c + 1) * chunk] * coef - m)
                total = p if total is None else total + p
                v = vc_ref[0, c * chunk : (c + 1) * chunk, :] if c < chunks else vn_ref[0]
                part = jnp.dot(p.astype(BF), v, preferred_element_type=F32)
                acc = part if acc is None else acc + part
            total = jnp.sum(total, axis=1, keepdims=True)
            out_ref[0:rows, h * HEAD_DIM : (h + 1) * HEAD_DIM] = (acc / total).astype(BF)
            level = m + jnp.log2(total)
            for part in range(3):
                piece = level.astype(BF).astype(F32)
                level = level - piece
                stats = jnp.where(lane == 3 * h + part, piece, stats)
        out_ref[rows : rows + 16, :] = stats.T[0:16, :].astype(BF)


def attend(first, info, qa, qb, cache_kv, new_kv):
    rows = qa.shape[0]
    cache_rows, new_rows = cache_kv.shape[1], new_kv.shape[1]
    keys = cache_rows + new_rows
    whole = pl.BlockSpec((rows, 2 * HEAD_DIM), lambda i, t: (0, 0))
    result = pl.BlockSpec((rows + 16, 2 * HEAD_DIM), lambda i, t: (0, 0))
    shape = jax.ShapeDtypeStruct((rows + 16, 2 * HEAD_DIM), BF)
    return pl.pallas_call(
        functools.partial(attn_kernel, first),
        grid_spec=pltpu.PrefetchScalarGridSpec(
            num_scalar_prefetch=1,
            grid=(1,),
            in_specs=[
                whole,
                whole,
                pl.BlockSpec((1, cache_rows, HEAD_DIM), lambda i, t: (0, 0, t[0])),
                pl.BlockSpec((1, cache_rows, HEAD_DIM), lambda i, t: (1, 0, t[0])),
                pl.BlockSpec((1, new_rows, HEAD_DIM), lambda i, t: (0, 0, t[0])),
                pl.BlockSpec((1, new_rows, HEAD_DIM), lambda i, t: (1, 0, t[0])),
            ],
            out_specs=[result, result],
            scratch_shapes=[pltpu.VMEM((4, rows, keys), F32)],
        ),
        out_shape=[shape, shape],
        compiler_params=pltpu.CompilerParams(vmem_limit_bytes=20 << 20),
        cost_estimate=pl.CostEstimate(
            flops=32 * rows * keys * HEAD_DIM,
            bytes_accessed=4 * keys * HEAD_DIM,
            transcendentals=4 * rows * keys,
        ),
        name="attend",
    )(info, qa, qb, cache_kv, cache_kv, new_kv, new_kv)


def project_kernel(a_ref, b_ref, c_ref, d_ref, w_ref, out_ref, att_ref):
    parts = (a_ref, b_ref, c_ref, d_ref)
    rows = out_ref.shape[0]
    pad = jnp.zeros((112, rows), F32)
    stats = [
        jnp.concatenate([p[rows : rows + 16, :].astype(F32), pad], axis=0).T for p in parts
    ]
    for h in range(2):
        cols = slice(h * HEAD_DIM, (h + 1) * HEAD_DIM)
        at = 3 * h
        levels = [
            t[:, at : at + 1] + t[:, at + 1 : at + 2] + t[:, at + 2 : at + 3] for t in stats
        ]
        best = jnp.maximum(
            jnp.maximum(levels[0], levels[1]), jnp.maximum(levels[2], levels[3])
        )
        weights = [jnp.exp2(v - best) for v in levels]
        total = weights[0] + weights[1] + weights[2] + weights[3]
        acc = None
        for w, p in zip(weights, parts):
            term = p[0:rows, cols].astype(F32) * w
            acc = term if acc is None else acc + term
        att_ref[:, cols] = (acc / total).astype(BF)
    out_ref[...] = jnp.dot(att_ref[...], w_ref[...], preferred_element_type=F32).astype(BF)


def project(parts, out_proj):
    rows, depth = parts[0].shape[0] - 16, parts[0].shape[1]
    width = out_proj.shape[1]
    return pl.pallas_call(
        project_kernel,
        in_specs=[pl.BlockSpec(memory_space=pltpu.VMEM)] * 5,
        out_specs=pl.BlockSpec(memory_space=pltpu.VMEM),
        out_shape=jax.ShapeDtypeStruct((rows, width), BF),
        scratch_shapes=[pltpu.VMEM((rows, depth), BF)],
        compiler_params=pltpu.CompilerParams(vmem_limit_bytes=16 << 20),
        cost_estimate=pl.CostEstimate(
            flops=2 * rows * depth * width, bytes_accessed=4 * depth * width, transcendentals=0
        ),
        name="project",
    )(*parts, out_proj)


def settle_kernel(arrived_ref, residual_ref, gain_ref, pick_ref, stream_ref, out_ref):
    tok, width = residual_ref.shape
    groups = arrived_ref.shape[0]
    chunk = out_ref.shape[2]
    chunks = width // chunk
    pieces = []
    square = None
    for c in range(chunks):
        cols = slice(c * chunk, (c + 1) * chunk)
        acc = arrived_ref[0, :, cols].astype(F32)
        for g in range(1, groups):
            acc = acc + arrived_ref[g, :, cols].astype(F32)
        stream = (residual_ref[:, cols].astype(F32) + acc).astype(BF)
        stream_ref[:, cols] = stream
        piece = stream.astype(F32)
        pieces.append(piece)
        term = jnp.sum(piece * piece, axis=1, keepdims=True)
        square = term if square is None else square + term
    scale = lax.rsqrt(square * (1.0 / width) + 1e-6)
    normed = [
        p * scale * gain_ref[:, c * chunk : (c + 1) * chunk] for c, p in enumerate(pieces)
    ]
    stacked = jnp.concatenate(normed, axis=0).astype(BF)
    rows = jnp.dot(pick_ref[...], stacked, preferred_element_type=F32).astype(BF)
    half = out_ref.shape[0] // 2
    rows = rows.reshape(half, 16, chunk)
    out_ref[0:half] = rows
    out_ref[half : 2 * half] = rows


def settle(arrived, residual, gain, pick):
    tok, width = residual.shape
    chunk = width // 4
    return pl.pallas_call(
        settle_kernel,
        out_shape=[
            jax.ShapeDtypeStruct((tok, width), BF),
            jax.ShapeDtypeStruct((pick.shape[0] // 8, 16, chunk), BF),
        ],
        compiler_params=pltpu.CompilerParams(vmem_limit_bytes=20 << 20),
        cost_estimate=pl.CostEstimate(
            flops=1 << 26, bytes_accessed=4 << 20, transcendentals=0
        ),
        name="settle",
    )(arrived, residual, gain.reshape(1, width), pick)


def expert_kernel(rows_ref, perm_ref, back_ref, win_ref, wout_ref, out_ref, x_ref, z_ref):
    chunk = rows_ref.shape[2]
    chunks = 4
    sources = rows_ref.shape[0]
    ff = wout_ref.shape[1]
    pieces = [(e, c) for e in range(2) for c in range(chunks)]
    for g in range(sources // 16):
        block = rows_ref[16 * g : 16 * g + 16].reshape(256, chunk)
        y = jnp.dot(perm_ref[...], block, preferred_element_type=F32).astype(BF)
        for i, (e, c) in enumerate(pieces):
            x_ref[e, g * 32 : g * 32 + 32, c * chunk : (c + 1) * chunk] = y[32 * i : 32 * i + 32]
    for e in range(2):
        both = jnp.concatenate([win_ref[e, 0], win_ref[e, 1]], axis=1)
        hidden = jnp.dot(x_ref[e], both, preferred_element_type=F32)
        gate, up = hidden[:, :ff], hidden[:, ff:]
        act = (gate / (1.0 + jnp.exp(-gate)) * up).astype(BF)
        z_ref[e] = jnp.dot(act, wout_ref[e], preferred_element_type=F32).astype(BF)
    for g in range(sources // 16):
        block = jnp.concatenate(
            [z_ref[e, g * 32 : g * 32 + 32, c * chunk : (c + 1) * chunk] for e, c in pieces],
            axis=0,
        )
        y = jnp.dot(back_ref[...], block, preferred_element_type=F32).astype(BF)
        out_ref[16 * g : 16 * g + 16] = y.reshape(16, 16, chunk)


def experts(rows, perm, back, w_in, w_out):
    sources, _, chunk = rows.shape
    width = 4 * chunk
    ff = w_out.shape[1]
    count = 2 * sources
    return pl.pallas_call(
        expert_kernel,
        in_specs=[pl.BlockSpec(memory_space=pltpu.VMEM)] * 5,
        out_specs=pl.BlockSpec(memory_space=pltpu.VMEM),
        out_shape=jax.ShapeDtypeStruct(rows.shape, BF),
        scratch_shapes=[
            pltpu.VMEM((2, count, width), BF),
            pltpu.VMEM((2, count, width), BF),
        ],
        compiler_params=pltpu.CompilerParams(vmem_limit_bytes=16 << 20),
        cost_estimate=pl.CostEstimate(
            flops=12 * count * width * ff,
            bytes_accessed=12 * width * ff,
            transcendentals=2 * count * ff,
        ),
        name="experts",
    )(rows, perm, back, w_in, w_out)


def combine_kernel(share_ref, returned_ref, stream_ref, out_ref):
    tok = stream_ref.shape[0]
    chunk = returned_ref.shape[1]
    both = jnp.dot(share_ref[...], returned_ref[...], preferred_element_type=F32)
    half = both.shape[0] // 2
    total = both[:half] + both[half:]
    for c in range(half // tok):
        cols = slice(c * chunk, (c + 1) * chunk)
        out_ref[:, cols] = (
            stream_ref[:, cols].astype(F32) + total[c * tok : (c + 1) * tok]
        ).astype(BF)


def combine(share, returned, stream):
    return pl.pallas_call(
        combine_kernel,
        out_shape=jax.ShapeDtypeStruct(stream.shape, BF),
        compiler_params=pltpu.CompilerParams(vmem_limit_bytes=20 << 20),
        name="combine",
    )(share, returned, stream)


def swap(v, axes, bit):
    count = 4 if len(axes) == 2 else 2
    return lax.ppermute(v, axes, [(i, i ^ bit) for i in range(count)])


def local(
    queries,
    new_kv,
    cache_kv,
    cached_len,
    image_spans,
    residual,
    out_proj,
    norm_gain,
    routes,
    gate_weights,
    w_in,
    w_out,
):
    seq = lax.axis_index(SEQ)
    tract = queries.shape[0]
    cache = cache_kv.shape[1]
    tok = residual.shape[0]
    width = residual.shape[1]
    quarter = width // 4
    spread = ("yh",) + MP

    query_parts = [queries] + [swap(queries, SEQ, d) for d in (1, 2, 3)]
    valid = jnp.clip(cached_len[0] - seq * cache, 0, cache)

    place = jnp.stack([lax.axis_index("x"), valid, seq]).astype(jnp.int32)
    info = jnp.concatenate([place, image_spans.reshape(-1)])

    def attend_pair(d):
        return attend(d, info, query_parts[d], query_parts[d + 1], cache_kv, new_kv)

    mine, beside = attend_pair(0)
    across, diagonal = attend_pair(2)
    parts = [mine, swap(beside, SEQ, 1), swap(across, SEQ, 2), swap(diagonal, SEQ, 3)]
    partial = project(parts, out_proj)
    partial, routes, gate_weights, w_in = lax.optimization_barrier(
        (partial, routes, gate_weights, w_in)
    )
    arrived = lax.all_to_all(
        partial.reshape(32, tok, width), MP, split_axis=0, concat_axis=0, tiled=True
    )
    turned = w_in.transpose(0, 2, 1, 3)

    gate_share = gate_weights / jnp.sum(gate_weights, axis=1, keepdims=True)
    top = routes.shape[1]
    same = routes[:, :, None, None] == routes[None, None, :, :]
    earlier = jnp.arange(tok)[:, None] > jnp.arange(tok)[None, :]
    rank = jnp.sum((same & earlier[:, None, :, None]).astype(jnp.int32), axis=(2, 3))
    slot = routes * 2 + rank
    pairs = 32
    placement = slot[:, :, None] == jnp.arange(pairs * 4, dtype=jnp.int32)[None, None, :]
    chosen = jnp.sum(placement.astype(F32), axis=1)
    weighed = jnp.sum(jnp.where(placement, gate_share[:, :, None], 0.0), axis=1)
    eye = jnp.eye(4, dtype=F32)

    def spread_rows(v):
        wide = v.reshape(1, tok, pairs, 1, 4) * eye.reshape(4, 1, 1, 4, 1)
        return wide.reshape(4 * tok, pairs * 16)

    pick = spread_rows(chosen).astype(BF).T
    share = spread_rows(weighed)
    coarse = share.astype(BF)
    fine = (share - coarse.astype(F32)).astype(BF)
    share = jnp.concatenate([coarse, fine], axis=0)
    share = jnp.concatenate([share, share], axis=1)

    perm = np.eye(256).reshape(16, 4, 2, 2, 256).transpose(2, 1, 0, 3, 4).reshape(256, 256)
    perm, back = jnp.asarray(perm, BF), jnp.asarray(perm.T, BF)

    arrived, pick, share, turned = lax.optimization_barrier((arrived, pick, share, turned))
    stream, outgoing = settle(arrived, residual, norm_gain, pick)

    own = lax.all_to_all(outgoing, spread, split_axis=0, concat_axis=0, tiled=True)
    other = swap(own, ("core",), 1)
    kept = experts(own, perm, back, turned, w_out)
    kept, other = lax.optimization_barrier((kept, other))
    sent = experts(other, perm, back, turned, w_out)
    got = swap(sent, ("core",), 1)
    summed = (kept.astype(F32) + got.astype(F32)).astype(BF)
    returned = lax.all_to_all(summed, spread, split_axis=0, concat_axis=0, tiled=True)
    return combine(share, returned.reshape(-1, quarter), stream)


def solution(mesh):
    fine = Mesh(mesh.devices.reshape(2, 2, 4, 2, 4), SEQ + MP)
    in_specs = (
        P(SEQ, MP),
        P(None, SEQ, None),
        P(None, SEQ, None),
        P(),
        P(),
        P(SEQ + MP, None),
        P(MP, None),
        P(),
        P(SEQ + MP, None),
        P(SEQ + MP, None),
        P(MP, None, None, SEQ),
        P(MP, SEQ, None),
    )
    return jax.shard_map(
        local, mesh=fine, in_specs=in_specs, out_specs=P(SEQ + MP, None), check_vma=False
    )
```

```python
import functools
import math

import jax
import jax.numpy as jnp
import numpy as np
from jax import lax
from jax.experimental import pallas as pl
from jax.experimental.pallas import tpu as pltpu
from jax.sharding import Mesh, PartitionSpec as P

HEAD_DIM = 128
SEQ = ("yh", "core")
MP = ("x", "yl", "z")
NEG = -1e30
BF = jnp.bfloat16
F32 = jnp.float32
ANY_LAST = (((1,), (1,)), ((), ()))


def attn_kernel(
    first, info, spans, qa_ref, qb_ref, kc_ref, vc_ref, kn_ref, vn_ref, oa_ref, ob_ref, s_ref
):
    rows = qa_ref.shape[0]
    chunk = kn_ref.shape[1]
    chunks = kc_ref.shape[1] // chunk
    coef = math.log2(math.e) / math.sqrt(HEAD_DIM)
    valid = info[1]
    key_pos = info[2] * rows + lax.broadcasted_iota(jnp.int32, (1, chunk), 1)
    lane = lax.broadcasted_iota(jnp.int32, (rows, 128), 1)
    column = lax.broadcasted_iota(jnp.int32, (1, chunk), 1)
    for b, (q_ref, out_ref) in enumerate(((qa_ref, oa_ref), (qb_ref, ob_ref))):
        pos = (info[2] ^ (first + b)) * rows + lax.broadcasted_iota(jnp.int32, (rows, 1), 0)
        limit = pos
        for a in range(3):
            start, end = spans[0, a], spans[1, a]
            limit = jnp.where((pos >= start) & (pos < end), jnp.maximum(limit, end - 1), limit)
        tract_ok = key_pos <= limit
        stats = jnp.zeros((rows, 128), F32)
        for h in range(2):
            at = 2 * b + h
            q = q_ref[:, h * HEAD_DIM : (h + 1) * HEAD_DIM]
            top = None
            for c in range(chunks + 1):
                k = kc_ref[0, c * chunk : (c + 1) * chunk, :] if c < chunks else kn_ref[0]
                s = lax.dot_general(q, k, ANY_LAST, preferred_element_type=F32)
                if c < chunks:
                    s = s + jnp.where(column < valid - c * chunk, 0.0, NEG)
                else:
                    s = jnp.where(tract_ok, s, NEG)
                s_ref[at, :, c * chunk : (c + 1) * chunk] = s
                top = s if top is None else jnp.maximum(top, s)
            m = jnp.max(top, axis=1, keepdims=True) * coef
            total = None
            acc = None
            for c in range(chunks + 1):
                p = jnp.exp2(s_ref[at, :, c * chunk : (c + 1) * chunk] * coef - m)
                total = p if total is None else total + p
                v = vc_ref[0, c * chunk : (c + 1) * chunk, :] if c < chunks else vn_ref[0]
                part = jnp.dot(p.astype(BF), v, preferred_element_type=F32)
                acc = part if acc is None else acc + part
            total = jnp.sum(total, axis=1, keepdims=True)
            out_ref[0:rows, h * HEAD_DIM : (h + 1) * HEAD_DIM] = (acc / total).astype(BF)
            level = m + jnp.log2(total)
            for part in range(3):
                piece = level.astype(BF).astype(F32)
                level = level - piece
                stats = jnp.where(lane == 3 * h + part, piece, stats)
        out_ref[rows : rows + 16, :] = stats.T[0:16, :].astype(BF)


def attend(first, info, spans, qa, qb, cache_kv, new_kv):
    rows = qa.shape[0]
    cache_rows, new_rows = cache_kv.shape[1], new_kv.shape[1]
    keys = cache_rows + new_rows
    whole = pl.BlockSpec((rows, 2 * HEAD_DIM), lambda i, t, u: (0, 0))
    result = pl.BlockSpec((rows + 16, 2 * HEAD_DIM), lambda i, t, u: (0, 0))
    shape = jax.ShapeDtypeStruct((rows + 16, 2 * HEAD_DIM), BF)
    return pl.pallas_call(
        functools.partial(attn_kernel, first),
        grid_spec=pltpu.PrefetchScalarGridSpec(
            num_scalar_prefetch=2,
            grid=(1,),
            in_specs=[
                whole,
                whole,
                pl.BlockSpec((1, cache_rows, HEAD_DIM), lambda i, t, u: (0, 0, t[0])),
                pl.BlockSpec((1, cache_rows, HEAD_DIM), lambda i, t, u: (1, 0, t[0])),
                pl.BlockSpec((1, new_rows, HEAD_DIM), lambda i, t, u: (0, 0, t[0])),
                pl.BlockSpec((1, new_rows, HEAD_DIM), lambda i, t, u: (1, 0, t[0])),
            ],
            out_specs=[result, result],
            scratch_shapes=[pltpu.VMEM((4, rows, keys), F32)],
        ),
        out_shape=[shape, shape],
        compiler_params=pltpu.CompilerParams(vmem_limit_bytes=50 << 20),
        cost_estimate=pl.CostEstimate(
            flops=32 * rows * keys * HEAD_DIM,
            bytes_accessed=4 * keys * HEAD_DIM,
            transcendentals=4 * rows * keys,
        ),
        name="attend",
    )(info, spans, qa, qb, cache_kv, cache_kv, new_kv, new_kv)


def project_kernel(a_ref, b_ref, c_ref, d_ref, w_ref, out_ref, att_ref):
    parts = (a_ref, b_ref, c_ref, d_ref)
    rows = out_ref.shape[0]
    pad = jnp.zeros((112, rows), F32)
    stats = [
        jnp.concatenate([p[rows : rows + 16, :].astype(F32), pad], axis=0).T for p in parts
    ]
    for h in range(2):
        cols = slice(h * HEAD_DIM, (h + 1) * HEAD_DIM)
        at = 3 * h
        levels = [
            t[:, at : at + 1] + t[:, at + 1 : at + 2] + t[:, at + 2 : at + 3] for t in stats
        ]
        best = jnp.maximum(
            jnp.maximum(levels[0], levels[1]), jnp.maximum(levels[2], levels[3])
        )
        weights = [jnp.exp2(v - best) for v in levels]
        total = weights[0] + weights[1] + weights[2] + weights[3]
        acc = None
        for w, p in zip(weights, parts):
            term = p[0:rows, cols].astype(F32) * w
            acc = term if acc is None else acc + term
        att_ref[:, cols] = (acc / total).astype(BF)
    out_ref[...] = jnp.dot(att_ref[...], w_ref[...], preferred_element_type=F32).astype(BF)


def project(parts, out_proj):
    rows, depth = parts[0].shape[0] - 16, parts[0].shape[1]
    width = out_proj.shape[1]
    return pl.pallas_call(
        project_kernel,
        in_specs=[pl.BlockSpec(memory_space=pltpu.VMEM)] * 5,
        out_specs=pl.BlockSpec(memory_space=pltpu.VMEM),
        out_shape=jax.ShapeDtypeStruct((rows, width), BF),
        scratch_shapes=[pltpu.VMEM((rows, depth), BF)],
        compiler_params=pltpu.CompilerParams(vmem_limit_bytes=16 << 20),
        cost_estimate=pl.CostEstimate(
            flops=2 * rows * depth * width, bytes_accessed=4 * depth * width, transcendentals=0
        ),
        name="project",
    )(*parts, out_proj)


def slot_table(flat, routes_ref, values, columns):
    tok, top = routes_ref.shape
    named = jnp.concatenate([routes_ref[...]] * 4, axis=0)
    row = lax.broadcasted_iota(jnp.int32, named.shape, 0)
    token = row & (tok - 1)
    rank = jnp.zeros(named.shape, jnp.int32)
    for t in range(tok):
        for k in range(top):
            rank = rank + jnp.where((named == flat[t, k]) & (token > t), 1, 0)
    slot = named * 2 + rank
    column = lax.broadcasted_iota(jnp.int32, (1, columns), 1)
    here = (column >> 4) * 4 + (column & 3)
    table = jnp.zeros((4 * tok, columns), F32)
    for k in range(top):
        value = values[:, k : k + 1] if values is not None else 1.0
        table = table + jnp.where(slot[:, k : k + 1] == here, value, 0.0)
    chunk = lax.broadcasted_iota(jnp.int32, (4 * tok, 1), 0) // tok
    return jnp.where(chunk == ((column >> 2) & 3), table, 0.0)


def settle_kernel(flat, arrived_ref, residual_ref, gain_ref, routes_ref, stream_ref, out_ref):
    tok, width = residual_ref.shape
    groups = arrived_ref.shape[0]
    chunk = out_ref.shape[2]
    chunks = width // chunk
    pieces = []
    square = None
    for c in range(chunks):
        cols = slice(c * chunk, (c + 1) * chunk)
        acc = arrived_ref[0, :, cols].astype(F32)
        for g in range(1, groups):
            acc = acc + arrived_ref[g, :, cols].astype(F32)
        stream = (residual_ref[:, cols].astype(F32) + acc).astype(BF)
        stream_ref[:, cols] = stream
        piece = stream.astype(F32)
        pieces.append(piece)
        term = jnp.sum(piece * piece, axis=1, keepdims=True)
        square = term if square is None else square + term
    scale = lax.rsqrt(square * (1.0 / width) + 1e-6)
    normed = [
        p * scale * gain_ref[:, c * chunk : (c + 1) * chunk] for c, p in enumerate(pieces)
    ]
    stacked = jnp.concatenate(normed, axis=0).astype(BF)
    half = out_ref.shape[0] // 2
    pick = slot_table(flat, routes_ref, None, half * 16).astype(BF)
    rows = lax.dot_general(
        pick, stacked, (((0,), (0,)), ((), ())), preferred_element_type=F32
    ).astype(BF)
    rows = rows.reshape(half, 16, chunk)
    out_ref[0:half] = rows
    out_ref[half : 2 * half] = rows


def settle(arrived, residual, gain, routes, devices):
    tok, width = residual.shape
    chunk = width // 4
    return pl.pallas_call(
        settle_kernel,
        in_specs=[pl.BlockSpec(memory_space=pltpu.SMEM)]
        + [pl.BlockSpec(memory_space=pltpu.VMEM)] * 4,
        out_specs=[pl.BlockSpec(memory_space=pltpu.VMEM)] * 2,
        out_shape=[
            jax.ShapeDtypeStruct((tok, width), BF),
            jax.ShapeDtypeStruct((devices, 16, chunk), BF),
        ],
        compiler_params=pltpu.CompilerParams(vmem_limit_bytes=10 << 20),
        cost_estimate=pl.CostEstimate(
            flops=1 << 26, bytes_accessed=4 << 20, transcendentals=0
        ),
        name="settle",
    )(routes, arrived, residual, gain.reshape(1, width), routes)


def expert_kernel(rows_ref, perm_ref, back_ref, win_ref, wout_ref, out_ref, x_ref, z_ref):
    chunk = rows_ref.shape[2]
    chunks = 4
    sources = rows_ref.shape[0]
    ff = wout_ref.shape[1]
    pieces = [(e, c) for e in range(2) for c in range(chunks)]
    for g in range(sources // 16):
        block = rows_ref[16 * g : 16 * g + 16].reshape(256, chunk)
        y = jnp.dot(perm_ref[...], block, preferred_element_type=F32).astype(BF)
        for i, (e, c) in enumerate(pieces):
            x_ref[e, g * 32 : g * 32 + 32, c * chunk : (c + 1) * chunk] = y[32 * i : 32 * i + 32]
    for e in range(2):
        both = jnp.concatenate([win_ref[e, 0], win_ref[e, 1]], axis=1)
        hidden = jnp.dot(x_ref[e], both, preferred_element_type=F32)
        gate, up = hidden[:, :ff], hidden[:, ff:]
        act = (gate / (1.0 + jnp.exp(-gate)) * up).astype(BF)
        z_ref[e] = jnp.dot(act, wout_ref[e], preferred_element_type=F32).astype(BF)
    for g in range(sources // 16):
        block = jnp.concatenate(
            [z_ref[e, g * 32 : g * 32 + 32, c * chunk : (c + 1) * chunk] for e, c in pieces],
            axis=0,
        )
        y = jnp.dot(back_ref[...], block, preferred_element_type=F32).astype(BF)
        out_ref[16 * g : 16 * g + 16] = y.reshape(16, 16, chunk)


def experts(rows, perm, back, w_in, w_out):
    sources, _, chunk = rows.shape
    width = 4 * chunk
    ff = w_out.shape[1]
    count = 2 * sources
    return pl.pallas_call(
        expert_kernel,
        in_specs=[pl.BlockSpec(memory_space=pltpu.VMEM)] * 5,
        out_specs=pl.BlockSpec(memory_space=pltpu.VMEM),
        out_shape=jax.ShapeDtypeStruct(rows.shape, BF),
        scratch_shapes=[
            pltpu.VMEM((2, count, width), BF),
            pltpu.VMEM((2, count, width), BF),
        ],
        compiler_params=pltpu.CompilerParams(vmem_limit_bytes=10 << 20),
        cost_estimate=pl.CostEstimate(
            flops=12 * count * width * ff,
            bytes_accessed=12 * width * ff,
            transcendentals=2 * count * ff,
        ),
        name="experts",
    )(rows, perm, back, w_in, w_out)


def combine_kernel(flat, routes_ref, gates_ref, returned_ref, stream_ref, out_ref):
    tok = stream_ref.shape[0]
    chunk = returned_ref.shape[1]
    gates = gates_ref[...]
    gates = gates / jnp.sum(gates, axis=1, keepdims=True)
    share = slot_table(
        flat, routes_ref, jnp.concatenate([gates] * 4, axis=0), returned_ref.shape[0] // 2
    )
    coarse = share.astype(BF).astype(F32)
    pieces = jnp.concatenate([coarse, share - coarse], axis=0).astype(BF)
    pieces = jnp.concatenate([pieces, pieces], axis=1)
    both = jnp.dot(pieces, returned_ref[...], preferred_element_type=F32)
    half = both.shape[0] // 2
    total = both[:half] + both[half:]
    for c in range(half // tok):
        cols = slice(c * chunk, (c + 1) * chunk)
        out_ref[:, cols] = (
            stream_ref[:, cols].astype(F32) + total[c * tok : (c + 1) * tok]
        ).astype(BF)


def combine(routes, gates, returned, stream):
    return pl.pallas_call(
        combine_kernel,
        in_specs=[pl.BlockSpec(memory_space=pltpu.SMEM)]
        + [pl.BlockSpec(memory_space=pltpu.VMEM)] * 4,
        out_specs=pl.BlockSpec(memory_space=pltpu.VMEM),
        out_shape=jax.ShapeDtypeStruct(stream.shape, BF),
        compiler_params=pltpu.CompilerParams(vmem_limit_bytes=10 << 20),
        name="combine",
    )(routes, routes, gates, returned, stream)


def swap(v, axes, bit):
    count = 4 if len(axes) == 2 else 2
    return lax.ppermute(v, axes, [(i, i ^ bit) for i in range(count)])


def local(
    queries,
    new_kv,
    cache_kv,
    cached_len,
    image_spans,
    residual,
    out_proj,
    norm_gain,
    routes,
    gate_weights,
    w_in,
    w_out,
):
    seq = lax.axis_index(SEQ)
    tract = queries.shape[0]
    cache = cache_kv.shape[1]
    tok = residual.shape[0]
    width = residual.shape[1]
    quarter = width // 4
    spread = ("yh",) + MP

    query_parts = [queries] + [swap(queries, SEQ, d) for d in (1, 2, 3)]
    valid = jnp.clip(cached_len[0] - seq * cache, 0, cache)

    info = jnp.stack([lax.axis_index("x"), valid, seq]).astype(jnp.int32)
    spans = image_spans.T

    def attend_pair(d):
        return attend(d, info, spans, query_parts[d], query_parts[d + 1], cache_kv, new_kv)

    mine, beside = attend_pair(0)
    mine, query_parts[2], query_parts[3] = lax.optimization_barrier(
        (mine, query_parts[2], query_parts[3])
    )
    across, diagonal = attend_pair(2)
    across, diagonal, w_in = lax.optimization_barrier((across, diagonal, w_in))
    turned = w_in.transpose(0, 2, 1, 3)
    parts = [mine, swap(beside, SEQ, 1), swap(across, SEQ, 2), swap(diagonal, SEQ, 3)]
    parts, turned = lax.optimization_barrier((parts, turned))
    partial = project(parts, out_proj)
    arrived = lax.all_to_all(
        partial.reshape(32, tok, width), MP, split_axis=0, concat_axis=0, tiled=True
    )

    perm = np.eye(256).reshape(16, 4, 2, 2, 256).transpose(2, 1, 0, 3, 4).reshape(256, 256)
    perm, back = jnp.asarray(perm, BF), jnp.asarray(perm.T, BF)

    stream, outgoing = settle(arrived, residual, norm_gain, routes, 64)

    own = lax.all_to_all(outgoing, spread, split_axis=0, concat_axis=0, tiled=True)
    other = swap(own, ("core",), 1)
    kept = experts(own, perm, back, turned, w_out)
    kept, other = lax.optimization_barrier((kept, other))
    sent = experts(other, perm, back, turned, w_out)
    got = swap(sent, ("core",), 1)
    summed = (kept.astype(F32) + got.astype(F32)).astype(BF)
    returned = lax.all_to_all(summed, spread, split_axis=0, concat_axis=0, tiled=True)
    return combine(routes, gate_weights, returned.reshape(-1, quarter), stream)


def solution(mesh):
    fine = Mesh(mesh.devices.reshape(2, 2, 4, 2, 4), SEQ + MP)
    in_specs = (
        P(SEQ, MP),
        P(None, SEQ, None),
        P(None, SEQ, None),
        P(),
        P(),
        P(SEQ + MP, None),
        P(MP, None),
        P(),
        P(SEQ + MP, None),
        P(SEQ + MP, None),
        P(MP, None, None, SEQ),
        P(MP, SEQ, None),
    )
    return jax.shard_map(
        local, mesh=fine, in_specs=in_specs, out_specs=P(SEQ + MP, None), check_vma=False
    )
```

```python
import functools
import math

import jax
import jax.numpy as jnp
import numpy as np
from jax import lax
from jax.experimental import pallas as pl
from jax.experimental.pallas import tpu as pltpu
from jax.sharding import Mesh, PartitionSpec as P

HEAD_DIM = 128
SEQ = ("yh", "core")
MP = ("x", "yl", "zh", "zl")
NEG = -1e30
BF = jnp.bfloat16
F32 = jnp.float32
ANY_LAST = (((1,), (1,)), ((), ()))


def attn_kernel(
    first, info, spans, qa_ref, qb_ref, kc_ref, vc_ref, kn_ref, vn_ref, oa_ref, ob_ref, s_ref
):
    rows = qa_ref.shape[0]
    heads = qa_ref.shape[1] // HEAD_DIM
    cache_rows = kc_ref.shape[1]
    chunk = kn_ref.shape[1]
    chunks = cache_rows // chunk
    coef = math.log2(math.e) / math.sqrt(HEAD_DIM)
    valid = info[1]
    key_pos = info[2] * chunk + lax.broadcasted_iota(jnp.int32, (1, chunk), 1)
    lane = lax.broadcasted_iota(jnp.int32, (rows, 128), 1)
    column = lax.broadcasted_iota(jnp.int32, (1, chunk), 1)
    row = lax.broadcasted_iota(jnp.int32, (2 * rows, 1), 0) & (rows - 1)
    for b, (q_ref, out_ref) in enumerate(((qa_ref, oa_ref), (qb_ref, ob_ref))):
        pos = (info[2] ^ (first + b)) * chunk + row + (row & ~7) + info[3] * 8
        limit = pos
        for a in range(3):
            start, end = spans[0, a], spans[1, a]
            limit = jnp.where((pos >= start) & (pos < end), jnp.maximum(limit, end - 1), limit)
        tract_ok = key_pos <= limit
        stats = jnp.zeros((rows, 128), F32)
        for pair in range(heads // 2):
            at = heads // 2 * b + pair
            cols = [
                slice((2 * pair + j) * HEAD_DIM, (2 * pair + j + 1) * HEAD_DIM) for j in range(2)
            ]
            q = jnp.concatenate([q_ref[:, cols[0]], q_ref[:, cols[1]]], axis=0)
            top = None
            for c in range(chunks + 1):
                if c < chunks:
                    k = kc_ref[0, c * chunk : (c + 1) * chunk, :]
                    s = lax.dot_general(q, k, ANY_LAST, preferred_element_type=F32)
                    s = s + jnp.where(column < valid - c * chunk, 0.0, NEG)
                else:
                    s = lax.dot_general(q, kn_ref[0], ANY_LAST, preferred_element_type=F32)
                    s = jnp.where(tract_ok, s, NEG)
                s_ref[at, :, c * chunk : (c + 1) * chunk] = s
                top = s if top is None else jnp.maximum(top, s)
            m = jnp.max(top, axis=1, keepdims=True) * coef
            total = None
            acc = None
            for c in range(chunks + 1):
                p = jnp.exp2(s_ref[at, :, c * chunk : (c + 1) * chunk] * coef - m)
                total = p if total is None else total + p
                v = vc_ref[0, c * chunk : (c + 1) * chunk, :] if c < chunks else vn_ref[0]
                part = jnp.dot(p.astype(BF), v, preferred_element_type=F32)
                acc = part if acc is None else acc + part
            total = jnp.sum(total, axis=1, keepdims=True)
            result = (acc / total).astype(BF)
            level = m + jnp.log2(total)
            for j in range(2):
                out_ref[0:rows, cols[j]] = result[j * rows : (j + 1) * rows]
                rest = level[j * rows : (j + 1) * rows]
                for part in range(3):
                    piece = rest.astype(BF).astype(F32)
                    rest = rest - piece
                    stats = jnp.where(lane == 3 * (2 * pair + j) + part, piece, stats)
        turned = stats.T[0:16, :].astype(BF)
        out_ref[rows : rows + 16, 0:rows] = turned
        out_ref[rows : rows + 16, rows:] = jnp.zeros((16, out_ref.shape[1] - rows), BF)


def attend(first, info, spans, qa, qb, cache_kv, new_kv):
    rows, width = qa.shape
    cache_rows, new_rows = cache_kv.shape[1], new_kv.shape[1]
    keys = cache_rows + new_rows
    whole = pl.BlockSpec((rows, width), lambda i, t, u: (0, 0))
    result = pl.BlockSpec((rows + 16, width), lambda i, t, u: (0, 0))
    shape = jax.ShapeDtypeStruct((rows + 16, width), BF)
    heads = width // HEAD_DIM
    return pl.pallas_call(
        functools.partial(attn_kernel, first),
        grid_spec=pltpu.PrefetchScalarGridSpec(
            num_scalar_prefetch=2,
            grid=(1,),
            in_specs=[
                whole,
                whole,
                pl.BlockSpec((1, cache_rows, HEAD_DIM), lambda i, t, u: (0, 0, t[0])),
                pl.BlockSpec((1, cache_rows, HEAD_DIM), lambda i, t, u: (1, 0, t[0])),
                pl.BlockSpec((1, new_rows, HEAD_DIM), lambda i, t, u: (0, 0, t[0])),
                pl.BlockSpec((1, new_rows, HEAD_DIM), lambda i, t, u: (1, 0, t[0])),
            ],
            out_specs=[result, result],
            scratch_shapes=[pltpu.VMEM((heads, 2 * rows, keys), F32)],
        ),
        out_shape=[shape, shape],
        compiler_params=pltpu.CompilerParams(vmem_limit_bytes=48 << 20),
        cost_estimate=pl.CostEstimate(
            flops=8 * heads * rows * keys * HEAD_DIM,
            bytes_accessed=4 * keys * HEAD_DIM,
            transcendentals=2 * heads * rows * keys,
        ),
        name="attend",
    )(info, spans, qa, qb, cache_kv, cache_kv, new_kv, new_kv)


def merge_kernel(a_ref, b_ref, c_ref, d_ref, out_ref):
    parts = (a_ref, b_ref, c_ref, d_ref)
    rows, heads = out_ref.shape[0], a_ref.shape[1] // HEAD_DIM
    pad = jnp.zeros((112, rows), F32)
    stats = [
        jnp.concatenate([p[rows : rows + 16, 0:rows].astype(F32), pad], axis=0).T for p in parts
    ]
    for h in range(heads):
        cols = slice(h * HEAD_DIM, (h + 1) * HEAD_DIM)
        at = 3 * h
        levels = [
            t[:, at : at + 1] + t[:, at + 1 : at + 2] + t[:, at + 2 : at + 3] for t in stats
        ]
        best = jnp.maximum(jnp.maximum(levels[0], levels[1]), jnp.maximum(levels[2], levels[3]))
        weights = [jnp.exp2(v - best) for v in levels]
        total = weights[0] + weights[1] + weights[2] + weights[3]
        acc = None
        for w, p in zip(weights, parts):
            term = p[0:rows, cols].astype(F32) * w
            acc = term if acc is None else acc + term
        out_ref[:, cols] = (acc / total).astype(BF)


def merge(parts):
    rows, depth = parts[0].shape[0] - 16, parts[0].shape[1]
    return pl.pallas_call(
        merge_kernel,
        in_specs=[pl.BlockSpec(memory_space=pltpu.VMEM)] * 4,
        out_specs=pl.BlockSpec(memory_space=pltpu.VMEM),
        out_shape=jax.ShapeDtypeStruct((rows, depth), BF),
        compiler_params=pltpu.CompilerParams(vmem_limit_bytes=10 << 20),
        cost_estimate=pl.CostEstimate(flops=1 << 20, bytes_accessed=5 << 17, transcendentals=0),
        name="merge",
    )(*parts)


def project_kernel(core_ref, mine_ref, other_ref, own_ref, near_ref, out_ref):
    rows = mine_ref.shape[0]
    half = own_ref.shape[0]
    core = core_ref[0]
    for att, side in ((mine_ref, core), (other_ref, 1 - core)):
        at = pl.multiple_of(side * rows, rows)
        out_ref[pl.ds(at, rows), :] = (
            jnp.dot(att[:, :half], own_ref[...], preferred_element_type=F32)
            + jnp.dot(att[:, half:], near_ref[...], preferred_element_type=F32)
        ).astype(BF)


def project(core, mine, other, own, near):
    rows, depth = mine.shape
    width = own.shape[1]
    return pl.pallas_call(
        project_kernel,
        in_specs=[pl.BlockSpec(memory_space=pltpu.SMEM)]
        + [pl.BlockSpec(memory_space=pltpu.VMEM)] * 4,
        out_specs=pl.BlockSpec(memory_space=pltpu.VMEM),
        out_shape=jax.ShapeDtypeStruct((2 * rows, width), BF),
        compiler_params=pltpu.CompilerParams(vmem_limit_bytes=10 << 20),
        cost_estimate=pl.CostEstimate(
            flops=4 * rows * depth * width, bytes_accessed=2 * depth * width, transcendentals=0
        ),
        name="project",
    )(core.reshape(1), mine, other, own, near)


def slot_table(flat, routes_ref, values, columns):
    tok, top = routes_ref.shape
    named = jnp.concatenate([routes_ref[...]] * 4, axis=0)
    row = lax.broadcasted_iota(jnp.int32, named.shape, 0)
    token = row & (tok - 1)
    rank = jnp.zeros(named.shape, jnp.int32)
    for t in range(tok):
        for k in range(top):
            rank = rank + jnp.where((named == flat[t, k]) & (token > t), 1, 0)
    slot = named * 2 + rank
    column = lax.broadcasted_iota(jnp.int32, (1, columns), 1)
    here = (column >> 4) * 4 + (column & 3)
    table = jnp.zeros((4 * tok, columns), F32)
    for k in range(top):
        value = values[:, k : k + 1] if values is not None else 1.0
        table = table + jnp.where(slot[:, k : k + 1] == here, value, 0.0)
    chunk = lax.broadcasted_iota(jnp.int32, (4 * tok, 1), 0) // tok
    return jnp.where(chunk == ((column >> 2) & 3), table, 0.0)


def tables_kernel(flat, routes_ref, gates_ref, pick_ref, share_ref):
    gates = gates_ref[...]
    gates = gates / jnp.sum(gates, axis=1, keepdims=True)
    columns = pick_ref.shape[1]
    pick_ref[...] = slot_table(flat, routes_ref, None, columns).astype(BF)
    share = slot_table(flat, routes_ref, jnp.concatenate([gates] * 4, axis=0), columns)
    coarse = share.astype(BF).astype(F32)
    pieces = jnp.concatenate([coarse, share - coarse], axis=0).astype(BF)
    share_ref[:, :columns] = pieces
    share_ref[:, columns:] = pieces


def tables(routes, gates, columns):
    rows = 4 * routes.shape[0]
    return pl.pallas_call(
        tables_kernel,
        in_specs=[pl.BlockSpec(memory_space=pltpu.SMEM)]
        + [pl.BlockSpec(memory_space=pltpu.VMEM)] * 2,
        out_specs=[pl.BlockSpec(memory_space=pltpu.VMEM)] * 2,
        out_shape=[
            jax.ShapeDtypeStruct((rows, columns), BF),
            jax.ShapeDtypeStruct((2 * rows, 2 * columns), BF),
        ],
        compiler_params=pltpu.CompilerParams(vmem_limit_bytes=10 << 20),
        name="tables",
    )(routes, routes, gates)


def settle_kernel(arrived_ref, residual_ref, gain_ref, pick_ref, stream_ref, out_ref):
    tok, width = residual_ref.shape
    groups = arrived_ref.shape[0]
    chunk = out_ref.shape[2]
    chunks = width // chunk
    pieces = []
    square = None
    for c in range(chunks):
        cols = slice(c * chunk, (c + 1) * chunk)
        first = 0 if c < chunks // 2 else groups // 2
        part = slice(c % 2 * chunk, (c % 2 + 1) * chunk)
        acc = arrived_ref[first, :, part].astype(F32)
        for g in range(first + 1, first + groups // 2):
            acc = acc + arrived_ref[g, :, part].astype(F32)
        stream = (residual_ref[:, cols].astype(F32) + acc).astype(BF)
        stream_ref[:, cols] = stream
        piece = stream.astype(F32)
        pieces.append(piece)
        term = jnp.sum(piece * piece, axis=1, keepdims=True)
        square = term if square is None else square + term
    scale = lax.rsqrt(square * (1.0 / width) + 1e-6)
    normed = [
        p * scale * gain_ref[:, c * chunk : (c + 1) * chunk] for c, p in enumerate(pieces)
    ]
    stacked = jnp.concatenate(normed, axis=0).astype(BF)
    half = out_ref.shape[0] // 2
    rows = lax.dot_general(
        pick_ref[...], stacked, (((0,), (0,)), ((), ())), preferred_element_type=F32
    ).astype(BF)
    rows = rows.reshape(half, 16, chunk)
    out_ref[0:half] = rows
    out_ref[half : 2 * half] = rows


def settle(arrived, residual, gain, pick):
    tok, width = residual.shape
    chunk = width // 4
    return pl.pallas_call(
        settle_kernel,
        in_specs=[pl.BlockSpec(memory_space=pltpu.VMEM)] * 4,
        out_specs=[pl.BlockSpec(memory_space=pltpu.VMEM)] * 2,
        out_shape=[
            jax.ShapeDtypeStruct((tok, width), BF),
            jax.ShapeDtypeStruct((pick.shape[1] // 8, 16, chunk), BF),
        ],
        compiler_params=pltpu.CompilerParams(vmem_limit_bytes=10 << 20),
        cost_estimate=pl.CostEstimate(
            flops=1 << 26, bytes_accessed=4 << 20, transcendentals=0
        ),
        name="settle",
    )(arrived, residual, gain.reshape(1, width), pick)


def expert_kernel(rows_ref, perm_ref, back_ref, win_ref, wout_ref, out_ref, x_ref, z_ref):
    chunk = rows_ref.shape[2]
    chunks = 4
    sources = rows_ref.shape[0]
    ff = wout_ref.shape[1]
    pieces = [(e, c) for e in range(2) for c in range(chunks)]
    for g in range(sources // 16):
        block = rows_ref[16 * g : 16 * g + 16].reshape(256, chunk)
        y = jnp.dot(perm_ref[...], block, preferred_element_type=F32).astype(BF)
        for i, (e, c) in enumerate(pieces):
            x_ref[e, g * 32 : g * 32 + 32, c * chunk : (c + 1) * chunk] = y[32 * i : 32 * i + 32]
    for e in range(2):
        both = jnp.concatenate([win_ref[e, 0], win_ref[e, 1]], axis=1)
        hidden = jnp.dot(x_ref[e], both, preferred_element_type=F32)
        gate, up = hidden[:, :ff], hidden[:, ff:]
        act = (gate / (1.0 + jnp.exp(-gate)) * up).astype(BF)
        z_ref[e] = jnp.dot(act, wout_ref[e], preferred_element_type=F32).astype(BF)
    for g in range(sources // 16):
        block = jnp.concatenate(
            [z_ref[e, g * 32 : g * 32 + 32, c * chunk : (c + 1) * chunk] for e, c in pieces],
            axis=0,
        )
        y = jnp.dot(back_ref[...], block, preferred_element_type=F32).astype(BF)
        out_ref[16 * g : 16 * g + 16] = y.reshape(16, 16, chunk)


def experts(rows, perm, back, w_in, w_out):
    sources, _, chunk = rows.shape
    width = 4 * chunk
    ff = w_out.shape[1]
    count = 2 * sources
    return pl.pallas_call(
        expert_kernel,
        in_specs=[pl.BlockSpec(memory_space=pltpu.VMEM)] * 5,
        out_specs=pl.BlockSpec(memory_space=pltpu.VMEM),
        out_shape=jax.ShapeDtypeStruct(rows.shape, BF),
        scratch_shapes=[
            pltpu.VMEM((2, count, width), BF),
            pltpu.VMEM((2, count, width), BF),
        ],
        compiler_params=pltpu.CompilerParams(vmem_limit_bytes=10 << 20),
        cost_estimate=pl.CostEstimate(
            flops=12 * count * width * ff,
            bytes_accessed=12 * width * ff,
            transcendentals=2 * count * ff,
        ),
        name="experts",
    )(rows, perm, back, w_in, w_out)


def combine_kernel(share_ref, returned_ref, stream_ref, out_ref):
    tok = stream_ref.shape[0]
    chunk = returned_ref.shape[1]
    both = jnp.dot(share_ref[...], returned_ref[...], preferred_element_type=F32)
    half = both.shape[0] // 2
    total = both[:half] + both[half:]
    for c in range(half // tok):
        cols = slice(c * chunk, (c + 1) * chunk)
        out_ref[:, cols] = (
            stream_ref[:, cols].astype(F32) + total[c * tok : (c + 1) * tok]
        ).astype(BF)


def combine(share, returned, stream):
    return pl.pallas_call(
        combine_kernel,
        in_specs=[pl.BlockSpec(memory_space=pltpu.VMEM)] * 3,
        out_specs=pl.BlockSpec(memory_space=pltpu.VMEM),
        out_shape=jax.ShapeDtypeStruct(stream.shape, BF),
        compiler_params=pltpu.CompilerParams(vmem_limit_bytes=10 << 20),
        name="combine",
    )(share, returned, stream)


def swap(v, axes, bit):
    count = 4 if len(axes) == 2 else 2
    return lax.ppermute(v, axes, [(i, i ^ bit) for i in range(count)])


def local(
    queries,
    new_kv,
    cache_kv,
    cached_len,
    image_spans,
    residual,
    out_proj,
    norm_gain,
    routes,
    gate_weights,
    w_in,
    w_out,
):
    seq = lax.axis_index(SEQ)
    tract = queries.shape[0]
    cache = cache_kv.shape[1]
    tok = residual.shape[0]
    width = residual.shape[1]
    quarter = width // 4
    spread = ("yh",) + MP

    core, parity = lax.axis_index("core"), lax.axis_index("zl")
    blocks = queries.reshape(tract // (2 * tok), 2, tok, queries.shape[1])
    stay = lax.dynamic_index_in_dim(blocks, parity, 1, keepdims=False)
    leave = lax.dynamic_index_in_dim(blocks, 1 - parity, 1, keepdims=False)
    rows = tract // 2
    came = swap(leave.reshape(rows, -1), ("zl",), 1)
    mine_q = jnp.concatenate([stay.reshape(rows, -1), came], axis=1)
    columns = lax.dynamic_slice_in_dim(out_proj, core * (width // 2), width // 2, 1)
    columns, mine_q = lax.optimization_barrier((columns, mine_q))
    near = swap(columns, ("zl",), 1)

    query_parts = [mine_q] + [swap(mine_q, SEQ, d) for d in (1, 2, 3)]
    valid = jnp.clip(cached_len[0] - seq * cache, 0, cache)

    info = jnp.stack([lax.axis_index("x"), valid, seq, parity]).astype(jnp.int32)
    spans = image_spans.T

    def attend_pair(d):
        return attend(d, info, spans, query_parts[d], query_parts[d + 1], cache_kv, new_kv)

    mine, beside = attend_pair(0)
    mine, query_parts[2], query_parts[3] = lax.optimization_barrier(
        (mine, query_parts[2], query_parts[3])
    )
    across, diagonal = attend_pair(2)
    across, diagonal, w_in, routes, gate_weights = lax.optimization_barrier(
        (across, diagonal, w_in, routes, gate_weights)
    )
    turned = w_in.transpose(0, 2, 1, 3)
    pick, share = tables(routes, gate_weights, 512)
    parts = [mine, swap(beside, SEQ, 1), swap(across, SEQ, 2), swap(diagonal, SEQ, 3)]
    parts, turned, pick, share = lax.optimization_barrier((parts, turned, pick, share))
    merged = merge(parts)
    partial = project(core, merged, swap(merged, ("core",), 1), columns, near)
    arrived = lax.all_to_all(
        partial.reshape(32, tok, width // 2),
        ("core", "x", "yl", "zh"),
        split_axis=0,
        concat_axis=0,
        tiled=True,
    )

    perm = np.eye(256).reshape(16, 4, 2, 2, 256).transpose(2, 1, 0, 3, 4).reshape(256, 256)
    perm, back = jnp.asarray(perm, BF), jnp.asarray(perm.T, BF)

    stream, outgoing = settle(arrived, residual, norm_gain, pick)

    own = lax.all_to_all(outgoing, spread, split_axis=0, concat_axis=0, tiled=True)
    other = swap(own, ("core",), 1)
    kept = experts(own, perm, back, turned, w_out)
    kept, other = lax.optimization_barrier((kept, other))
    sent = experts(other, perm, back, turned, w_out)
    got = swap(sent, ("core",), 1)
    summed = (kept.astype(F32) + got.astype(F32)).astype(BF)
    returned = lax.all_to_all(summed, spread, split_axis=0, concat_axis=0, tiled=True)
    return combine(share, returned.reshape(-1, quarter), stream)


def solution(mesh):
    fine = Mesh(mesh.devices.reshape(2, 2, 4, 2, 2, 2), SEQ + MP)
    in_specs = (
        P(SEQ, MP),
        P(None, SEQ, None),
        P(None, SEQ, None),
        P(),
        P(),
        P(SEQ + MP, None),
        P(MP, None),
        P(),
        P(SEQ + MP, None),
        P(SEQ + MP, None),
        P(MP, None, None, SEQ),
        P(MP, SEQ, None),
    )
    return jax.shard_map(
        local, mesh=fine, in_specs=in_specs, out_specs=P(SEQ + MP, None), check_vma=False
    )
```

```python
import functools
import math

import jax
import jax.numpy as jnp
import numpy as np
from jax import lax
from jax.experimental import pallas as pl
from jax.experimental.pallas import tpu as pltpu
from jax.sharding import Mesh, PartitionSpec as P

HEAD_DIM = 128
SEQ = ("yh", "core")
MP = ("x", "yl", "zh", "zl")
NEG = -1e30
BF = jnp.bfloat16
F32 = jnp.float32
ANY_LAST = (((1,), (1,)), ((), ()))


def attn_kernel(
    first, info, spans, qa_ref, qb_ref, kc_ref, vc_ref, kn_ref, vn_ref, oa_ref, ob_ref, s_ref
):
    rows = qa_ref.shape[0]
    heads = qa_ref.shape[1] // HEAD_DIM
    cache_rows = kc_ref.shape[1]
    chunk = kn_ref.shape[1]
    chunks = cache_rows // chunk
    coef = math.log2(math.e) / math.sqrt(HEAD_DIM)
    valid = info[1]
    key_pos = info[2] * chunk + lax.broadcasted_iota(jnp.int32, (1, chunk), 1)
    lane = lax.broadcasted_iota(jnp.int32, (rows, 128), 1)
    column = lax.broadcasted_iota(jnp.int32, (1, chunk), 1)
    row = lax.broadcasted_iota(jnp.int32, (2 * rows, 1), 0) & (rows - 1)
    for b, (q_ref, out_ref) in enumerate(((qa_ref, oa_ref), (qb_ref, ob_ref))):
        pos = (info[2] ^ (first + b)) * chunk + row + (row & ~7) + info[3] * 8
        limit = pos
        for a in range(3):
            start, end = spans[0, a], spans[1, a]
            limit = jnp.where((pos >= start) & (pos < end), jnp.maximum(limit, end - 1), limit)
        tract_ok = key_pos <= limit
        stats = jnp.zeros((rows, 128), F32)
        for pair in range(heads // 2):
            at = heads // 2 * b + pair
            cols = [
                slice((2 * pair + j) * HEAD_DIM, (2 * pair + j + 1) * HEAD_DIM) for j in range(2)
            ]
            q = jnp.concatenate([q_ref[:, cols[0]], q_ref[:, cols[1]]], axis=0)
            top = None
            for c in range(chunks + 1):
                if c < chunks:
                    k = kc_ref[0, c * chunk : (c + 1) * chunk, :]
                    s = lax.dot_general(q, k, ANY_LAST, preferred_element_type=F32)
                    s = s + jnp.where(column < valid - c * chunk, 0.0, NEG)
                else:
                    s = lax.dot_general(q, kn_ref[0], ANY_LAST, preferred_element_type=F32)
                    s = jnp.where(tract_ok, s, NEG)
                s_ref[at, :, c * chunk : (c + 1) * chunk] = s
                top = s if top is None else jnp.maximum(top, s)
            m = jnp.max(top, axis=1, keepdims=True) * coef
            total = None
            acc = None
            for c in range(chunks + 1):
                p = jnp.exp2(s_ref[at, :, c * chunk : (c + 1) * chunk] * coef - m)
                total = p if total is None else total + p
                v = vc_ref[0, c * chunk : (c + 1) * chunk, :] if c < chunks else vn_ref[0]
                part = jnp.dot(p.astype(BF), v, preferred_element_type=F32)
                acc = part if acc is None else acc + part
            total = jnp.sum(total, axis=1, keepdims=True)
            result = (acc / total).astype(BF)
            level = m + jnp.log2(total)
            for j in range(2):
                out_ref[0:rows, cols[j]] = result[j * rows : (j + 1) * rows]
                rest = level[j * rows : (j + 1) * rows]
                for part in range(3):
                    piece = rest.astype(BF).astype(F32)
                    rest = rest - piece
                    stats = jnp.where(lane == 3 * (2 * pair + j) + part, piece, stats)
        turned = stats.T[0:16, :].astype(BF)
        out_ref[rows : rows + 16, 0:rows] = turned
        out_ref[rows : rows + 16, rows:] = jnp.zeros((16, out_ref.shape[1] - rows), BF)


def attend(first, info, spans, qa, qb, cache_kv, new_kv):
    rows, width = qa.shape
    cache_rows, new_rows = cache_kv.shape[1], new_kv.shape[1]
    keys = cache_rows + new_rows
    whole = pl.BlockSpec((rows, width), lambda i, t, u: (0, 0))
    result = pl.BlockSpec((rows + 16, width), lambda i, t, u: (0, 0))
    shape = jax.ShapeDtypeStruct((rows + 16, width), BF)
    heads = width // HEAD_DIM
    return pl.pallas_call(
        functools.partial(attn_kernel, first),
        grid_spec=pltpu.PrefetchScalarGridSpec(
            num_scalar_prefetch=2,
            grid=(1,),
            in_specs=[
                whole,
                whole,
                pl.BlockSpec((1, cache_rows, HEAD_DIM), lambda i, t, u: (0, 0, t[0])),
                pl.BlockSpec((1, cache_rows, HEAD_DIM), lambda i, t, u: (1, 0, t[0])),
                pl.BlockSpec((1, new_rows, HEAD_DIM), lambda i, t, u: (0, 0, t[0])),
                pl.BlockSpec((1, new_rows, HEAD_DIM), lambda i, t, u: (1, 0, t[0])),
            ],
            out_specs=[result, result],
            scratch_shapes=[pltpu.VMEM((heads, 2 * rows, keys), F32)],
        ),
        out_shape=[shape, shape],
        compiler_params=pltpu.CompilerParams(vmem_limit_bytes=48 << 20),
        cost_estimate=pl.CostEstimate(
            flops=8 * heads * rows * keys * HEAD_DIM,
            bytes_accessed=4 * keys * HEAD_DIM,
            transcendentals=2 * heads * rows * keys,
        ),
        name="attend",
    )(info, spans, qa, qb, cache_kv, cache_kv, new_kv, new_kv)


def merge_kernel(a_ref, b_ref, c_ref, d_ref, out_ref):
    parts = (a_ref, b_ref, c_ref, d_ref)
    rows, heads = out_ref.shape[0], a_ref.shape[1] // HEAD_DIM
    pad = jnp.zeros((112, rows), F32)
    stats = [
        jnp.concatenate([p[rows : rows + 16, 0:rows].astype(F32), pad], axis=0).T for p in parts
    ]
    for h in range(heads):
        cols = slice(h * HEAD_DIM, (h + 1) * HEAD_DIM)
        at = 3 * h
        levels = [
            t[:, at : at + 1] + t[:, at + 1 : at + 2] + t[:, at + 2 : at + 3] for t in stats
        ]
        best = jnp.maximum(jnp.maximum(levels[0], levels[1]), jnp.maximum(levels[2], levels[3]))
        weights = [jnp.exp2(v - best) for v in levels]
        total = weights[0] + weights[1] + weights[2] + weights[3]
        acc = None
        for w, p in zip(weights, parts):
            term = p[0:rows, cols].astype(F32) * w
            acc = term if acc is None else acc + term
        out_ref[:, cols] = (acc / total).astype(BF)


def merge(parts):
    rows, depth = parts[0].shape[0] - 16, parts[0].shape[1]
    return pl.pallas_call(
        merge_kernel,
        in_specs=[pl.BlockSpec(memory_space=pltpu.VMEM)] * 4,
        out_specs=pl.BlockSpec(memory_space=pltpu.VMEM),
        out_shape=jax.ShapeDtypeStruct((rows, depth), BF),
        compiler_params=pltpu.CompilerParams(vmem_limit_bytes=10 << 20),
        cost_estimate=pl.CostEstimate(flops=1 << 20, bytes_accessed=5 << 17, transcendentals=0),
        name="merge",
    )(*parts)


def project_kernel(core_ref, mine_ref, other_ref, own_ref, near_ref, out_ref):
    rows = mine_ref.shape[0]
    half = own_ref.shape[0]
    core = core_ref[0]
    for att, side in ((mine_ref, core), (other_ref, 1 - core)):
        at = pl.multiple_of(side * rows, rows)
        out_ref[pl.ds(at, rows), :] = (
            jnp.dot(att[:, :half], own_ref[...], preferred_element_type=F32)
            + jnp.dot(att[:, half:], near_ref[...], preferred_element_type=F32)
        ).astype(BF)


def project(core, mine, other, own, near):
    rows, depth = mine.shape
    width = own.shape[1]
    return pl.pallas_call(
        project_kernel,
        in_specs=[pl.BlockSpec(memory_space=pltpu.SMEM)]
        + [pl.BlockSpec(memory_space=pltpu.VMEM)] * 4,
        out_specs=pl.BlockSpec(memory_space=pltpu.VMEM),
        out_shape=jax.ShapeDtypeStruct((2 * rows, width), BF),
        compiler_params=pltpu.CompilerParams(vmem_limit_bytes=10 << 20),
        cost_estimate=pl.CostEstimate(
            flops=4 * rows * depth * width, bytes_accessed=2 * depth * width, transcendentals=0
        ),
        name="project",
    )(core.reshape(1), mine, other, own, near)


def slot_table(flat, routes_ref, values, columns):
    tok, top = routes_ref.shape
    named = jnp.concatenate([routes_ref[...]] * 4, axis=0)
    row = lax.broadcasted_iota(jnp.int32, named.shape, 0)
    token = row & (tok - 1)
    rank = jnp.zeros(named.shape, jnp.int32)
    for t in range(tok):
        for k in range(top):
            rank = rank + jnp.where((named == flat[t, k]) & (token > t), 1, 0)
    slot = named * 2 + rank
    column = lax.broadcasted_iota(jnp.int32, (1, columns), 1)
    here = (column >> 4) * 4 + (column & 3)
    table = jnp.zeros((4 * tok, columns), F32)
    for k in range(top):
        value = values[:, k : k + 1] if values is not None else 1.0
        table = table + jnp.where(slot[:, k : k + 1] == here, value, 0.0)
    chunk = lax.broadcasted_iota(jnp.int32, (4 * tok, 1), 0) // tok
    return jnp.where(chunk == ((column >> 2) & 3), table, 0.0)


def tables_kernel(flat, routes_ref, gates_ref, pick_ref, share_ref):
    gates = gates_ref[...]
    gates = gates / jnp.sum(gates, axis=1, keepdims=True)
    columns = pick_ref.shape[1]
    pick_ref[...] = slot_table(flat, routes_ref, None, columns).astype(BF)
    share = slot_table(flat, routes_ref, jnp.concatenate([gates] * 4, axis=0), columns)
    coarse = share.astype(BF).astype(F32)
    pieces = jnp.concatenate([coarse, share - coarse], axis=0).astype(BF)
    share_ref[:, :columns] = pieces
    share_ref[:, columns:] = pieces


def tables(routes, gates, columns):
    rows = 4 * routes.shape[0]
    return pl.pallas_call(
        tables_kernel,
        in_specs=[pl.BlockSpec(memory_space=pltpu.SMEM)]
        + [pl.BlockSpec(memory_space=pltpu.VMEM)] * 2,
        out_specs=[pl.BlockSpec(memory_space=pltpu.VMEM)] * 2,
        out_shape=[
            jax.ShapeDtypeStruct((rows, columns), BF),
            jax.ShapeDtypeStruct((2 * rows, 2 * columns), BF),
        ],
        compiler_params=pltpu.CompilerParams(vmem_limit_bytes=10 << 20),
        name="tables",
    )(routes, routes, gates)


def settle_kernel(arrived_ref, residual_ref, gain_ref, pick_ref, stream_ref, out_ref):
    tok, width = residual_ref.shape
    groups = arrived_ref.shape[0]
    chunk = out_ref.shape[2]
    chunks = width // chunk
    pieces = []
    square = None
    for c in range(chunks):
        cols = slice(c * chunk, (c + 1) * chunk)
        first = 0 if c < chunks // 2 else groups // 2
        part = slice(c % 2 * chunk, (c % 2 + 1) * chunk)
        acc = arrived_ref[first, :, part].astype(F32)
        for g in range(first + 1, first + groups // 2):
            acc = acc + arrived_ref[g, :, part].astype(F32)
        stream = (residual_ref[:, cols].astype(F32) + acc).astype(BF)
        stream_ref[:, cols] = stream
        piece = stream.astype(F32)
        pieces.append(piece)
        term = jnp.sum(piece * piece, axis=1, keepdims=True)
        square = term if square is None else square + term
    scale = lax.rsqrt(square * (1.0 / width) + 1e-6)
    normed = [
        p * scale * gain_ref[:, c * chunk : (c + 1) * chunk] for c, p in enumerate(pieces)
    ]
    stacked = jnp.concatenate(normed, axis=0).astype(BF)
    half = out_ref.shape[0] // 2
    rows = lax.dot_general(
        pick_ref[...], stacked, (((0,), (0,)), ((), ())), preferred_element_type=F32
    ).astype(BF)
    rows = rows.reshape(half, 16, chunk)
    out_ref[0:half] = rows
    out_ref[half : 2 * half] = rows


def settle(arrived, residual, gain, pick):
    tok, width = residual.shape
    chunk = width // 4
    return pl.pallas_call(
        settle_kernel,
        in_specs=[pl.BlockSpec(memory_space=pltpu.VMEM)] * 4,
        out_specs=[pl.BlockSpec(memory_space=pltpu.VMEM)] * 2,
        out_shape=[
            jax.ShapeDtypeStruct((tok, width), BF),
            jax.ShapeDtypeStruct((pick.shape[1] // 8, 16, chunk), BF),
        ],
        compiler_params=pltpu.CompilerParams(vmem_limit_bytes=10 << 20),
        cost_estimate=pl.CostEstimate(
            flops=1 << 26, bytes_accessed=4 << 20, transcendentals=0
        ),
        name="settle",
    )(arrived, residual, gain.reshape(1, width), pick)


def expert_kernel(rows_ref, perm_ref, back_ref, win_ref, wout_ref, out_ref, x_ref, z_ref):
    chunk = rows_ref.shape[2]
    chunks = 4
    sources = rows_ref.shape[0]
    ff = wout_ref.shape[1]
    pieces = [(e, c) for e in range(2) for c in range(chunks)]
    for g in range(sources // 16):
        block = rows_ref[16 * g : 16 * g + 16].reshape(256, chunk)
        y = jnp.dot(perm_ref[...], block, preferred_element_type=F32).astype(BF)
        for i, (e, c) in enumerate(pieces):
            x_ref[e, g * 32 : g * 32 + 32, c * chunk : (c + 1) * chunk] = y[32 * i : 32 * i + 32]
    for e in range(2):
        both = jnp.concatenate([win_ref[e, 0], win_ref[e, 1]], axis=1)
        hidden = jnp.dot(x_ref[e], both, preferred_element_type=F32)
        gate, up = hidden[:, :ff], hidden[:, ff:]
        act = (gate / (1.0 + jnp.exp(-gate)) * up).astype(BF)
        z_ref[e] = jnp.dot(act, wout_ref[e], preferred_element_type=F32).astype(BF)
    for g in range(sources // 16):
        block = jnp.concatenate(
            [z_ref[e, g * 32 : g * 32 + 32, c * chunk : (c + 1) * chunk] for e, c in pieces],
            axis=0,
        )
        y = jnp.dot(back_ref[...], block, preferred_element_type=F32).astype(BF)
        out_ref[16 * g : 16 * g + 16] = y.reshape(16, 16, chunk)


def experts(rows, perm, back, w_in, w_out):
    sources, _, chunk = rows.shape
    width = 4 * chunk
    ff = w_out.shape[1]
    count = 2 * sources
    return pl.pallas_call(
        expert_kernel,
        in_specs=[pl.BlockSpec(memory_space=pltpu.VMEM)] * 5,
        out_specs=pl.BlockSpec(memory_space=pltpu.VMEM),
        out_shape=jax.ShapeDtypeStruct(rows.shape, BF),
        scratch_shapes=[
            pltpu.VMEM((2, count, width), BF),
            pltpu.VMEM((2, count, width), BF),
        ],
        compiler_params=pltpu.CompilerParams(vmem_limit_bytes=10 << 20),
        cost_estimate=pl.CostEstimate(
            flops=12 * count * width * ff,
            bytes_accessed=12 * width * ff,
            transcendentals=2 * count * ff,
        ),
        name="experts",
    )(rows, perm, back, w_in, w_out)


def combine_kernel(share_ref, returned_ref, stream_ref, out_ref):
    tok = stream_ref.shape[0]
    chunk = returned_ref.shape[1]
    both = jnp.dot(share_ref[...], returned_ref[...], preferred_element_type=F32)
    half = both.shape[0] // 2
    total = both[:half] + both[half:]
    for c in range(half // tok):
        cols = slice(c * chunk, (c + 1) * chunk)
        out_ref[:, cols] = (
            stream_ref[:, cols].astype(F32) + total[c * tok : (c + 1) * tok]
        ).astype(BF)


def combine(share, returned, stream):
    return pl.pallas_call(
        combine_kernel,
        in_specs=[pl.BlockSpec(memory_space=pltpu.VMEM)] * 3,
        out_specs=pl.BlockSpec(memory_space=pltpu.VMEM),
        out_shape=jax.ShapeDtypeStruct(stream.shape, BF),
        compiler_params=pltpu.CompilerParams(vmem_limit_bytes=10 << 20),
        name="combine",
    )(share, returned, stream)


def swap(v, axes, bit):
    count = 4 if len(axes) == 2 else 2
    return lax.ppermute(v, axes, [(i, i ^ bit) for i in range(count)])


def local(
    queries,
    new_kv,
    cache_kv,
    cached_len,
    image_spans,
    residual,
    out_proj,
    norm_gain,
    routes,
    gate_weights,
    w_in,
    w_out,
):
    seq = lax.axis_index(SEQ)
    tract = queries.shape[0]
    cache = cache_kv.shape[1]
    tok = residual.shape[0]
    width = residual.shape[1]
    quarter = width // 4
    spread = ("yh",) + MP

    core, parity = lax.axis_index("core"), lax.axis_index("zl")
    blocks = queries.reshape(tract // (2 * tok), 2, tok, queries.shape[1])
    stay = lax.dynamic_index_in_dim(blocks, parity, 1, keepdims=False)
    leave = lax.dynamic_index_in_dim(blocks, 1 - parity, 1, keepdims=False)
    rows = tract // 2
    came = swap(leave.reshape(rows, -1), ("zl",), 1)
    mine_q = jnp.concatenate([stay.reshape(rows, -1), came], axis=1)
    columns = lax.dynamic_slice_in_dim(out_proj, core * (width // 2), width // 2, 1)
    columns, mine_q = lax.optimization_barrier((columns, mine_q))
    near = swap(columns, ("zl",), 1)

    query_parts = [mine_q] + [swap(mine_q, SEQ, d) for d in (1, 2, 3)]
    valid = jnp.clip(cached_len[0] - seq * cache, 0, cache)

    info = jnp.stack([lax.axis_index("x"), valid, seq, parity]).astype(jnp.int32)
    spans = image_spans.T

    def attend_pair(d):
        return attend(d, info, spans, query_parts[d], query_parts[d + 1], cache_kv, new_kv)

    mine, beside = attend_pair(0)
    mine, query_parts[2], query_parts[3] = lax.optimization_barrier(
        (mine, query_parts[2], query_parts[3])
    )
    across, diagonal = attend_pair(2)
    across, diagonal, w_in = lax.optimization_barrier((across, diagonal, w_in))
    turned = w_in.transpose(0, 2, 1, 3)
    parts = [mine, swap(beside, SEQ, 1), swap(across, SEQ, 2), swap(diagonal, SEQ, 3)]
    parts, turned = lax.optimization_barrier((parts, turned))
    merged, routes, gate_weights = lax.optimization_barrier(
        (merge(parts), routes, gate_weights)
    )
    beside_merged = swap(merged, ("core",), 1)
    pick, share = tables(routes, gate_weights, 512)
    beside_merged, pick, share = lax.optimization_barrier((beside_merged, pick, share))
    partial = project(core, merged, beside_merged, columns, near)
    arrived = lax.all_to_all(
        partial.reshape(32, tok, width // 2),
        ("core", "x", "yl", "zh"),
        split_axis=0,
        concat_axis=0,
        tiled=True,
    )

    perm = np.eye(256).reshape(16, 4, 2, 2, 256).transpose(2, 1, 0, 3, 4).reshape(256, 256)
    perm, back = jnp.asarray(perm, BF), jnp.asarray(perm.T, BF)

    stream, outgoing = settle(arrived, residual, norm_gain, pick)

    own = lax.all_to_all(outgoing, spread, split_axis=0, concat_axis=0, tiled=True)
    other = swap(own, ("core",), 1)
    kept = experts(own, perm, back, turned, w_out)
    kept, other = lax.optimization_barrier((kept, other))
    sent = experts(other, perm, back, turned, w_out)
    got = swap(sent, ("core",), 1)
    summed = (kept.astype(F32) + got.astype(F32)).astype(BF)
    returned = lax.all_to_all(summed, spread, split_axis=0, concat_axis=0, tiled=True)
    return combine(share, returned.reshape(-1, quarter), stream)


def solution(mesh):
    fine = Mesh(mesh.devices.reshape(2, 2, 4, 2, 2, 2), SEQ + MP)
    in_specs = (
        P(SEQ, MP),
        P(None, SEQ, None),
        P(None, SEQ, None),
        P(),
        P(),
        P(SEQ + MP, None),
        P(MP, None),
        P(),
        P(SEQ + MP, None),
        P(SEQ + MP, None),
        P(MP, None, None, SEQ),
        P(MP, SEQ, None),
    )
    return jax.shard_map(
        local, mesh=fine, in_specs=in_specs, out_specs=P(SEQ + MP, None), check_vma=False
    )
```

```python
import functools
import math

import jax
import jax.numpy as jnp
import numpy as np
from jax import lax
from jax.experimental import pallas as pl
from jax.experimental.pallas import tpu as pltpu
from jax.sharding import Mesh, PartitionSpec as P

HEAD_DIM = 128
SEQ = ("yh", "core")
MP = ("x", "yl", "zh", "zl")
NEG = -1e30
BF = jnp.bfloat16
F32 = jnp.float32
ANY_LAST = (((1,), (1,)), ((), ()))


def attn_kernel(
    first, info, spans, qa_ref, qb_ref, kc_ref, vc_ref, kn_ref, vn_ref, oa_ref, ob_ref, s_ref
):
    rows = qa_ref.shape[0]
    heads = qa_ref.shape[1] // HEAD_DIM
    cache_rows = kc_ref.shape[1]
    chunk = kn_ref.shape[1]
    chunks = cache_rows // chunk
    coef = math.log2(math.e) / math.sqrt(HEAD_DIM)
    valid = info[1]
    key_pos = info[2] * chunk + lax.broadcasted_iota(jnp.int32, (1, chunk), 1)
    lane = lax.broadcasted_iota(jnp.int32, (rows, 128), 1)
    column = lax.broadcasted_iota(jnp.int32, (1, chunk), 1)
    row = lax.broadcasted_iota(jnp.int32, (2 * rows, 1), 0) & (rows - 1)
    for b, (q_ref, out_ref) in enumerate(((qa_ref, oa_ref), (qb_ref, ob_ref))):
        pos = (info[2] ^ (first + b)) * chunk + row + (row & ~7) + info[3] * 8
        limit = pos
        for a in range(3):
            start, end = spans[0, a], spans[1, a]
            limit = jnp.where((pos >= start) & (pos < end), jnp.maximum(limit, end - 1), limit)
        tract_ok = key_pos <= limit
        stats = jnp.zeros((rows, 128), F32)
        for pair in range(heads // 2):
            at = heads // 2 * b + pair
            cols = [
                slice((2 * pair + j) * HEAD_DIM, (2 * pair + j + 1) * HEAD_DIM) for j in range(2)
            ]
            q = jnp.concatenate([q_ref[:, cols[0]], q_ref[:, cols[1]]], axis=0)
            top = None
            for c in range(chunks + 1):
                if c < chunks:
                    k = kc_ref[0, c * chunk : (c + 1) * chunk, :]
                    s = lax.dot_general(q, k, ANY_LAST, preferred_element_type=F32)
                    s = s + jnp.where(column < valid - c * chunk, 0.0, NEG)
                else:
                    s = lax.dot_general(q, kn_ref[0], ANY_LAST, preferred_element_type=F32)
                    s = jnp.where(tract_ok, s, NEG)
                s_ref[at, :, c * chunk : (c + 1) * chunk] = s
                top = s if top is None else jnp.maximum(top, s)
            m = jnp.max(top, axis=1, keepdims=True) * coef
            total = None
            acc = None
            for c in range(chunks + 1):
                p = jnp.exp2(s_ref[at, :, c * chunk : (c + 1) * chunk] * coef - m)
                total = p if total is None else total + p
                v = vc_ref[0, c * chunk : (c + 1) * chunk, :] if c < chunks else vn_ref[0]
                part = jnp.dot(p.astype(BF), v, preferred_element_type=F32)
                acc = part if acc is None else acc + part
            total = jnp.sum(total, axis=1, keepdims=True)
            result = (acc / total).astype(BF)
            level = m + jnp.log2(total)
            for j in range(2):
                out_ref[0:rows, cols[j]] = result[j * rows : (j + 1) * rows]
                rest = level[j * rows : (j + 1) * rows]
                for part in range(3):
                    piece = rest.astype(BF).astype(F32)
                    rest = rest - piece
                    stats = jnp.where(lane == 3 * (2 * pair + j) + part, piece, stats)
        turned = stats.T[0:16, :].astype(BF)
        out_ref[rows : rows + 16, 0:rows] = turned
        out_ref[rows : rows + 16, rows:] = jnp.zeros((16, out_ref.shape[1] - rows), BF)


def attend(first, info, spans, qa, qb, cache_kv, new_kv):
    rows, width = qa.shape
    cache_rows, new_rows = cache_kv.shape[1], new_kv.shape[1]
    keys = cache_rows + new_rows
    whole = pl.BlockSpec((rows, width), lambda i, t, u: (0, 0))
    result = pl.BlockSpec((rows + 16, width), lambda i, t, u: (0, 0))
    shape = jax.ShapeDtypeStruct((rows + 16, width), BF)
    heads = width // HEAD_DIM
    return pl.pallas_call(
        functools.partial(attn_kernel, first),
        grid_spec=pltpu.PrefetchScalarGridSpec(
            num_scalar_prefetch=2,
            grid=(1,),
            in_specs=[
                whole,
                whole,
                pl.BlockSpec((1, cache_rows, HEAD_DIM), lambda i, t, u: (0, 0, t[0])),
                pl.BlockSpec((1, cache_rows, HEAD_DIM), lambda i, t, u: (1, 0, t[0])),
                pl.BlockSpec((1, new_rows, HEAD_DIM), lambda i, t, u: (0, 0, t[0])),
                pl.BlockSpec((1, new_rows, HEAD_DIM), lambda i, t, u: (1, 0, t[0])),
            ],
            out_specs=[result, result],
            scratch_shapes=[pltpu.VMEM((heads, 2 * rows, keys), F32)],
        ),
        out_shape=[shape, shape],
        compiler_params=pltpu.CompilerParams(vmem_limit_bytes=48 << 20),
        cost_estimate=pl.CostEstimate(
            flops=8 * heads * rows * keys * HEAD_DIM,
            bytes_accessed=4 * keys * HEAD_DIM,
            transcendentals=2 * heads * rows * keys,
        ),
        name="attend",
    )(info, spans, qa, qb, cache_kv, cache_kv, new_kv, new_kv)


def merge_kernel(a_ref, b_ref, c_ref, d_ref, out_ref):
    parts = (a_ref, b_ref, c_ref, d_ref)
    rows, heads = out_ref.shape[0], a_ref.shape[1] // HEAD_DIM
    pad = jnp.zeros((112, rows), F32)
    stats = [
        jnp.concatenate([p[rows : rows + 16, 0:rows].astype(F32), pad], axis=0).T for p in parts
    ]
    for h in range(heads):
        cols = slice(h * HEAD_DIM, (h + 1) * HEAD_DIM)
        at = 3 * h
        levels = [
            t[:, at : at + 1] + t[:, at + 1 : at + 2] + t[:, at + 2 : at + 3] for t in stats
        ]
        best = jnp.maximum(jnp.maximum(levels[0], levels[1]), jnp.maximum(levels[2], levels[3]))
        weights = [jnp.exp2(v - best) for v in levels]
        total = weights[0] + weights[1] + weights[2] + weights[3]
        acc = None
        for w, p in zip(weights, parts):
            term = p[0:rows, cols].astype(F32) * w
            acc = term if acc is None else acc + term
        out_ref[:, cols] = (acc / total).astype(BF)


def merge(parts):
    rows, depth = parts[0].shape[0] - 16, parts[0].shape[1]
    return pl.pallas_call(
        merge_kernel,
        in_specs=[pl.BlockSpec(memory_space=pltpu.VMEM)] * 4,
        out_specs=pl.BlockSpec(memory_space=pltpu.VMEM),
        out_shape=jax.ShapeDtypeStruct((rows, depth), BF),
        compiler_params=pltpu.CompilerParams(vmem_limit_bytes=10 << 20),
        cost_estimate=pl.CostEstimate(flops=1 << 20, bytes_accessed=5 << 17, transcendentals=0),
        name="merge",
    )(*parts)


def project_kernel(core_ref, mine_ref, other_ref, own_ref, near_ref, out_ref):
    rows = mine_ref.shape[0]
    half = own_ref.shape[0]
    core = core_ref[0]
    att = jnp.concatenate([mine_ref[...], other_ref[...]], axis=0)
    both = (
        jnp.dot(att[:, :half], own_ref[...], preferred_element_type=F32)
        + jnp.dot(att[:, half:], near_ref[...], preferred_element_type=F32)
    ).astype(BF)
    for part, side in ((both[:rows], core), (both[rows:], 1 - core)):
        out_ref[pl.ds(pl.multiple_of(side * rows, rows), rows), :] = part


def project(core, mine, other, own, near):
    rows, depth = mine.shape
    width = own.shape[1]
    return pl.pallas_call(
        project_kernel,
        in_specs=[pl.BlockSpec(memory_space=pltpu.SMEM)]
        + [pl.BlockSpec(memory_space=pltpu.VMEM)] * 4,
        out_specs=pl.BlockSpec(memory_space=pltpu.VMEM),
        out_shape=jax.ShapeDtypeStruct((2 * rows, width), BF),
        compiler_params=pltpu.CompilerParams(vmem_limit_bytes=10 << 20),
        cost_estimate=pl.CostEstimate(
            flops=4 * rows * depth * width, bytes_accessed=2 * depth * width, transcendentals=0
        ),
        name="project",
    )(core.reshape(1), mine, other, own, near)


def slot_table(flat, routes_ref, values, columns):
    tok, top = routes_ref.shape
    named = jnp.concatenate([routes_ref[...]] * 4, axis=0)
    row = lax.broadcasted_iota(jnp.int32, named.shape, 0)
    token = row & (tok - 1)
    rank = jnp.zeros(named.shape, jnp.int32)
    for t in range(tok):
        for k in range(top):
            rank = rank + jnp.where((named == flat[t, k]) & (token > t), 1, 0)
    slot = named * 2 + rank
    column = lax.broadcasted_iota(jnp.int32, (1, columns), 1)
    here = (column >> 4) * 4 + (column & 3)
    table = jnp.zeros((4 * tok, columns), F32)
    for k in range(top):
        value = values[:, k : k + 1] if values is not None else 1.0
        table = table + jnp.where(slot[:, k : k + 1] == here, value, 0.0)
    chunk = lax.broadcasted_iota(jnp.int32, (4 * tok, 1), 0) // tok
    return jnp.where(chunk == ((column >> 2) & 3), table, 0.0)


def tables_kernel(flat, routes_ref, gates_ref, pick_ref, share_ref):
    gates = gates_ref[...]
    gates = gates / jnp.sum(gates, axis=1, keepdims=True)
    columns = pick_ref.shape[1]
    pick_ref[...] = slot_table(flat, routes_ref, None, columns).astype(BF)
    share = slot_table(flat, routes_ref, jnp.concatenate([gates] * 4, axis=0), columns)
    coarse = share.astype(BF).astype(F32)
    pieces = jnp.concatenate([coarse, share - coarse], axis=0).astype(BF)
    share_ref[:, :columns] = pieces
    share_ref[:, columns:] = pieces


def tables(routes, gates, columns):
    rows = 4 * routes.shape[0]
    return pl.pallas_call(
        tables_kernel,
        in_specs=[pl.BlockSpec(memory_space=pltpu.SMEM)]
        + [pl.BlockSpec(memory_space=pltpu.VMEM)] * 2,
        out_specs=[pl.BlockSpec(memory_space=pltpu.VMEM)] * 2,
        out_shape=[
            jax.ShapeDtypeStruct((rows, columns), BF),
            jax.ShapeDtypeStruct((2 * rows, 2 * columns), BF),
        ],
        compiler_params=pltpu.CompilerParams(vmem_limit_bytes=10 << 20),
        name="tables",
    )(routes, routes, gates)


def settle_kernel(arrived_ref, residual_ref, gain_ref, pick_ref, stream_ref, out_ref):
    tok, width = residual_ref.shape
    groups = arrived_ref.shape[0]
    chunk = out_ref.shape[2]
    chunks = width // chunk
    pieces = []
    square = None
    for c in range(chunks):
        cols = slice(c * chunk, (c + 1) * chunk)
        first = 0 if c < chunks // 2 else groups // 2
        part = slice(c % 2 * chunk, (c % 2 + 1) * chunk)
        acc = arrived_ref[first, :, part].astype(F32)
        for g in range(first + 1, first + groups // 2):
            acc = acc + arrived_ref[g, :, part].astype(F32)
        stream = (residual_ref[:, cols].astype(F32) + acc).astype(BF)
        stream_ref[:, cols] = stream
        piece = stream.astype(F32)
        pieces.append(piece)
        term = jnp.sum(piece * piece, axis=1, keepdims=True)
        square = term if square is None else square + term
    scale = lax.rsqrt(square * (1.0 / width) + 1e-6)
    normed = [
        p * scale * gain_ref[:, c * chunk : (c + 1) * chunk] for c, p in enumerate(pieces)
    ]
    stacked = jnp.concatenate(normed, axis=0).astype(BF)
    half = out_ref.shape[0] // 2
    rows = lax.dot_general(
        pick_ref[...], stacked, (((0,), (0,)), ((), ())), preferred_element_type=F32
    ).astype(BF)
    rows = rows.reshape(half, 16, chunk)
    out_ref[0:half] = rows
    out_ref[half : 2 * half] = rows


def settle(arrived, residual, gain, pick):
    tok, width = residual.shape
    chunk = width // 4
    return pl.pallas_call(
        settle_kernel,
        in_specs=[pl.BlockSpec(memory_space=pltpu.VMEM)] * 4,
        out_specs=[pl.BlockSpec(memory_space=pltpu.VMEM)] * 2,
        out_shape=[
            jax.ShapeDtypeStruct((tok, width), BF),
            jax.ShapeDtypeStruct((pick.shape[1] // 8, 16, chunk), BF),
        ],
        compiler_params=pltpu.CompilerParams(vmem_limit_bytes=10 << 20),
        cost_estimate=pl.CostEstimate(
            flops=1 << 26, bytes_accessed=4 << 20, transcendentals=0
        ),
        name="settle",
    )(arrived, residual, gain.reshape(1, width), pick)


def expert_kernel(rows_ref, perm_ref, back_ref, win_ref, wout_ref, out_ref, x_ref, z_ref):
    chunk = rows_ref.shape[2]
    chunks = 4
    sources = rows_ref.shape[0]
    ff = wout_ref.shape[1]
    pieces = [(e, c) for e in range(2) for c in range(chunks)]
    for g in range(sources // 16):
        block = rows_ref[16 * g : 16 * g + 16].reshape(256, chunk)
        y = jnp.dot(perm_ref[...], block, preferred_element_type=F32).astype(BF)
        for i, (e, c) in enumerate(pieces):
            x_ref[e, g * 32 : g * 32 + 32, c * chunk : (c + 1) * chunk] = y[32 * i : 32 * i + 32]
    for e in range(2):
        both = jnp.concatenate([win_ref[e, 0], win_ref[e, 1]], axis=1)
        hidden = jnp.dot(x_ref[e], both, preferred_element_type=F32)
        gate, up = hidden[:, :ff], hidden[:, ff:]
        act = (gate / (1.0 + jnp.exp(-gate)) * up).astype(BF)
        z_ref[e] = jnp.dot(act, wout_ref[e], preferred_element_type=F32).astype(BF)
    for g in range(sources // 16):
        block = jnp.concatenate(
            [z_ref[e, g * 32 : g * 32 + 32, c * chunk : (c + 1) * chunk] for e, c in pieces],
            axis=0,
        )
        y = jnp.dot(back_ref[...], block, preferred_element_type=F32).astype(BF)
        out_ref[16 * g : 16 * g + 16] = y.reshape(16, 16, chunk)


def experts(rows, perm, back, w_in, w_out):
    sources, _, chunk = rows.shape
    width = 4 * chunk
    ff = w_out.shape[1]
    count = 2 * sources
    return pl.pallas_call(
        expert_kernel,
        in_specs=[pl.BlockSpec(memory_space=pltpu.VMEM)] * 5,
        out_specs=pl.BlockSpec(memory_space=pltpu.VMEM),
        out_shape=jax.ShapeDtypeStruct(rows.shape, BF),
        scratch_shapes=[
            pltpu.VMEM((2, count, width), BF),
            pltpu.VMEM((2, count, width), BF),
        ],
        compiler_params=pltpu.CompilerParams(vmem_limit_bytes=10 << 20),
        cost_estimate=pl.CostEstimate(
            flops=12 * count * width * ff,
            bytes_accessed=12 * width * ff,
            transcendentals=2 * count * ff,
        ),
        name="experts",
    )(rows, perm, back, w_in, w_out)


def combine_kernel(share_ref, returned_ref, stream_ref, out_ref):
    tok = stream_ref.shape[0]
    chunk = returned_ref.shape[1]
    both = jnp.dot(share_ref[...], returned_ref[...], preferred_element_type=F32)
    half = both.shape[0] // 2
    total = both[:half] + both[half:]
    for c in range(half // tok):
        cols = slice(c * chunk, (c + 1) * chunk)
        out_ref[:, cols] = (
            stream_ref[:, cols].astype(F32) + total[c * tok : (c + 1) * tok]
        ).astype(BF)


def combine(share, returned, stream):
    return pl.pallas_call(
        combine_kernel,
        in_specs=[pl.BlockSpec(memory_space=pltpu.VMEM)] * 3,
        out_specs=pl.BlockSpec(memory_space=pltpu.VMEM),
        out_shape=jax.ShapeDtypeStruct(stream.shape, BF),
        compiler_params=pltpu.CompilerParams(vmem_limit_bytes=10 << 20),
        name="combine",
    )(share, returned, stream)


def swap(v, axes, bit):
    count = 4 if len(axes) == 2 else 2
    return lax.ppermute(v, axes, [(i, i ^ bit) for i in range(count)])


def local(
    queries,
    new_kv,
    cache_kv,
    cached_len,
    image_spans,
    residual,
    out_proj,
    norm_gain,
    routes,
    gate_weights,
    w_in,
    w_out,
):
    seq = lax.axis_index(SEQ)
    tract = queries.shape[0]
    cache = cache_kv.shape[1]
    tok = residual.shape[0]
    width = residual.shape[1]
    quarter = width // 4
    spread = ("yh",) + MP

    core, parity = lax.axis_index("core"), lax.axis_index("zl")
    blocks = queries.reshape(tract // (2 * tok), 2, tok, queries.shape[1])
    stay = lax.dynamic_index_in_dim(blocks, parity, 1, keepdims=False)
    leave = lax.dynamic_index_in_dim(blocks, 1 - parity, 1, keepdims=False)
    rows = tract // 2
    came = swap(leave.reshape(rows, -1), ("zl",), 1)
    mine_q = jnp.concatenate([stay.reshape(rows, -1), came], axis=1)
    columns = lax.dynamic_slice_in_dim(out_proj, core * (width // 2), width // 2, 1)
    columns, mine_q = lax.optimization_barrier((columns, mine_q))
    near = swap(columns, ("zl",), 1)

    query_parts = [mine_q] + [swap(mine_q, SEQ, d) for d in (1, 2, 3)]
    valid = jnp.clip(cached_len[0] - seq * cache, 0, cache)

    info = jnp.stack([lax.axis_index("x"), valid, seq, parity]).astype(jnp.int32)
    spans = image_spans.T

    def attend_pair(d):
        return attend(d, info, spans, query_parts[d], query_parts[d + 1], cache_kv, new_kv)

    mine, beside = attend_pair(0)
    mine, query_parts[2], query_parts[3] = lax.optimization_barrier(
        (mine, query_parts[2], query_parts[3])
    )
    across, diagonal = attend_pair(2)
    across, diagonal, w_in = lax.optimization_barrier((across, diagonal, w_in))
    turned = w_in.transpose(0, 2, 1, 3)
    parts = [mine, swap(beside, SEQ, 1), swap(across, SEQ, 2), swap(diagonal, SEQ, 3)]
    parts, turned = lax.optimization_barrier((parts, turned))
    merged, routes, gate_weights = lax.optimization_barrier(
        (merge(parts), routes, gate_weights)
    )
    beside_merged = swap(merged, ("core",), 1)
    pick, share = tables(routes, gate_weights, 512)
    beside_merged, pick, share = lax.optimization_barrier((beside_merged, pick, share))
    partial = project(core, merged, beside_merged, columns, near)
    arrived = lax.all_to_all(
        partial.reshape(32, tok, width // 2),
        ("core", "x", "yl", "zh"),
        split_axis=0,
        concat_axis=0,
        tiled=True,
    )

    perm = np.eye(256).reshape(16, 4, 2, 2, 256).transpose(2, 1, 0, 3, 4).reshape(256, 256)
    perm, back = jnp.asarray(perm, BF), jnp.asarray(perm.T, BF)

    stream, outgoing = settle(arrived, residual, norm_gain, pick)

    own = lax.all_to_all(outgoing, spread, split_axis=0, concat_axis=0, tiled=True)
    other = swap(own, ("core",), 1)
    kept = experts(own, perm, back, turned, w_out)
    kept, other = lax.optimization_barrier((kept, other))
    sent = experts(other, perm, back, turned, w_out)
    got = swap(sent, ("core",), 1)
    summed = (kept.astype(F32) + got.astype(F32)).astype(BF)
    returned = lax.all_to_all(summed, spread, split_axis=0, concat_axis=0, tiled=True)
    return combine(share, returned.reshape(-1, quarter), stream)


def solution(mesh):
    fine = Mesh(mesh.devices.reshape(2, 2, 4, 2, 2, 2), SEQ + MP)
    in_specs = (
        P(SEQ, MP),
        P(None, SEQ, None),
        P(None, SEQ, None),
        P(),
        P(),
        P(SEQ + MP, None),
        P(MP, None),
        P(),
        P(SEQ + MP, None),
        P(SEQ + MP, None),
        P(MP, None, None, SEQ),
        P(MP, SEQ, None),
    )
    return jax.shard_map(
        local, mesh=fine, in_specs=in_specs, out_specs=P(SEQ + MP, None), check_vma=False
    )
```
